1024 devices in a mesh: group: 8 (over y), shard: 32 (over x, z_hi), mp: 4 (over z_lo, core).
Axes of the slice: x: 8, y: 8, z: 8 (z_hi: 4, z_lo: 2; z = z_hi * 2 + z_lo), core: 2. Of those that a mesh axis runs over, the one named last changes fastest.
Arguments:
- passage_states: bfloat16 [65536, 768], P(('group', 'shard', 'mp')), may hold values from -6 to 6
- query_emb: bfloat16 [8192, 768], P(('group', 'shard', 'mp')), may hold values from -82 to 82
- head_weight: bfloat16 [768, 768], replicated, may hold values from -0.21875 to 0.21875
- head_bias: float32 [768], replicated, may hold values from -4 to 4
- norm_gain: float32 [768], replicated, may hold values from 0.25 to 1.75
- candidate_ids: int32 [8192, 65], P(('group', 'shard', 'mp')), may hold values from 0 to 65535, as said below
Outputs:
- losses: float32 [8192], P(('group', 'shard', 'mp'))
- query_grad: float32 [8192, 768], P(('group', 'shard', 'mp'))
The draws below stay inside these ranges and needn't reach their ends.
Inputs may be any that keep to these rules, and one draw needn't show every extreme that they name: `candidate_ids`: index row r belongs to owner ((r // 64) // 4) % 32. Among the 520 candidates of the queries of one device, exactly 40 lie in the rows of one owner drawn from the seed, and the rest are spread as evenly as possible over the other owners; rows within an owner are drawn evenly and may repeat.
All inputs are finite; a program needn't handle non-finite values.
Results may differ from the reference program's by a relative error of at most 0.014.
Values may be sent and summed in bfloat16 or wider, within the bound.
A program may use at most 32 MiB of HBM per device.

```python
import math
import jax
import jax.numpy as jnp
from jax import lax

D = 768
RB = 64
Q_DEV = 8
CANDS = 65
CAP = 40
NP = 65536
NQ = 8192
SLAB = 2048
N_SHARD = 32
N_MP = 4


def draw_query_emb(key, part):
    key = jax.random.fold_in(key, 5)
    key_scale, key_base = jax.random.split(key)
    scales = jnp.exp(jax.random.uniform(key_scale, (NQ, 1), jnp.float32, 0.0, math.log(4.0)))
    base = jnp.clip(jax.random.normal(key_base, (NQ, D), jnp.float32), -6.0, 6.0)
    return (base * scales).astype(jnp.bfloat16)


def draw_candidate_ids(key, part):
    key = jax.random.fold_in(key, 11)
    devices = NQ // Q_DEV
    slot_count = Q_DEV * CANDS
    others_count = N_SHARD - 1

    def one_device(dev_key):
        key_hot, key_order, key_shuffle, key_rows = jax.random.split(dev_key, 4)
        hottest = jax.random.randint(key_hot, (), 0, N_SHARD)
        others = jax.random.permutation(key_order, others_count)
        others = others + (others >= hottest).astype(jnp.int32)
        remain = slot_count - CAP
        counts_other = remain // others_count + (jnp.arange(others_count) < remain % others_count).astype(jnp.int32)
        counts = jnp.concatenate([jnp.full((1,), CAP, jnp.int32), counts_other.astype(jnp.int32)])
        owner_list = jnp.concatenate([hottest.reshape(1).astype(jnp.int32), others.astype(jnp.int32)])
        bounds = jnp.cumsum(counts)
        places = jnp.arange(slot_count)
        which = jnp.sum((places[:, None] >= bounds[None, :]).astype(jnp.int32), axis=1)
        owners = jax.random.permutation(key_shuffle, owner_list[which])
        slab_row = jax.random.randint(key_rows, (slot_count,), 0, SLAB)
        group_of = slab_row // (N_MP * RB)
        part_of = slab_row // RB % N_MP
        within = slab_row % RB
        return (((group_of * N_SHARD + owners) * N_MP + part_of) * RB + within).astype(jnp.int32).reshape(Q_DEV, CANDS)
    return jax.vmap(one_device)(jax.random.split(key, devices)).reshape(NQ, CANDS)


def shard_levels(own_key, extent, pieces, least, top_value):
    factor_of, own = 1.0, jax.random.fold_in(own_key, 6)
    for dim, blocks in pieces:
        heights = jnp.exp(jax.random.uniform(jax.random.fold_in(own, dim), (blocks,), jnp.float32, least / len(pieces), top_value / len(pieces)))
        factor_of = factor_of * jnp.repeat(heights, extent[dim] // blocks).reshape([-1 if axis == dim else 1 for axis in range(len(extent))])
    return factor_of


def bell_draw(key, shape, scale, limit, pieces=(), dtype=jnp.bfloat16):
    factor_of = shard_levels(key, shape, pieces, -0.22, 0.18) if pieces else 1.0
    values = jax.random.normal(key, shape, jnp.float32) * scale * factor_of
    return jnp.minimum(jnp.maximum(values, -limit), limit).astype(dtype)


def setup_inputs(seed: int = 0) -> dict:
    arg_keys = jax.random.split(jax.random.key(seed), 7)
    passage_states = bell_draw(arg_keys[0], (NP, D), 1.0, 6.0, ((0, 1024),))
    query_emb = draw_query_emb(jax.random.fold_in(arg_keys[6], 71), 0)
    head_weight = bell_draw(arg_keys[2], (D, D), D ** -0.5, 0.21875)
    head_bias = bell_draw(arg_keys[3], (D,), 1.0, 4.0, (), jnp.float32)
    norm_gain = jnp.clip(1.0 + 0.15 * jax.random.normal(arg_keys[4], (D,), jnp.float32), 0.25, 1.75)
    candidate_ids = draw_candidate_ids(jax.random.fold_in(arg_keys[6], 71), 0)
    return {"passage_states": passage_states, "query_emb": query_emb, "head_weight": head_weight, "head_bias": head_bias, "norm_gain": norm_gain, "candidate_ids": candidate_ids}


def encode(states, weight, head_bias, gains):
    hidden = jnp.dot(states, weight, preferred_element_type=jnp.float32) + head_bias
    average = lax.optimization_barrier(jnp.mean(hidden, axis=-1, keepdims=True))
    centred = hidden - average
    spread = lax.optimization_barrier(jnp.mean(centred * centred, axis=-1, keepdims=True))
    return (centred * lax.rsqrt(spread + 1e-05) * gains).astype(jnp.bfloat16)

def reference(passage_states, query_emb, head_weight, head_bias, norm_gain, candidate_ids):
    index_rows = encode(passage_states, head_weight, head_bias, norm_gain)
    scaling = 1.0 / math.sqrt(D)
    width = math.gcd(NQ, 512)
    blocks = NQ // width

    def one_block(pair):
        queries, chosen = pair
        picked = index_rows[chosen].astype(jnp.float32)
        scores = jnp.einsum('qd,qcd->qc', queries.astype(jnp.float32), picked) * scaling
        highest = lax.optimization_barrier(jnp.max(scores, axis=1, keepdims=True))
        weights = jnp.exp(scores - highest)
        totals = lax.optimization_barrier(jnp.sum(weights, axis=1, keepdims=True))
        losses = highest[:, 0] + jnp.log(totals[:, 0]) - scores[:, 0]
        chances = weights / totals
        mean_row = jnp.einsum('qc,qcd->qd', chances, picked)
        gradient = (mean_row - picked[:, 0]) * scaling
        return (losses, gradient)
    losses, gradient = lax.map(one_block, (query_emb.reshape(blocks, width, D), candidate_ids.reshape(blocks, width, CANDS)))
    return (losses.reshape(NQ), gradient.reshape(NQ, D))
```

```python
import functools
import math

import jax
import jax.numpy as jnp
from jax import lax
from jax.experimental import pallas as pl
from jax.experimental.pallas import tpu as pltpu
from jax.sharding import PartitionSpec as P

MESH = pl.DeviceIdType.MESH
NT = (((1,), (1,)), ((), ()))
LOW = -1e30
REACH = ((4, 3), (3, 4), (4, 3))


def kernel(
    rings, owners, rows, queries,
    states, query, ids, bias, gain, w_hbm,
    stat_out, grad_out,
    w, slab, qbuf, qmat, idbuf, cnt, score, prob, part, parts, stat, stats, back,
    w_sem, ys, yr, zs, zr, cs, cr, qs, qr, ds, dr, ts, tr, ps, pr,
):
    width = states.shape[1]
    half_width = width // 2
    half = rows // 2
    span = 4 * rows
    scaling = 1.0 / math.sqrt(width)
    g, s, mp = lax.axis_index("group"), lax.axis_index("shard"), lax.axis_index("mp")
    right = {"group": lax.rem(g + 1, rings)}
    left = {"group": lax.rem(g + rings - 1, rings)}
    across = lax.rem(mp + 2, 4)
    twin = mp + 1 - 2 * lax.rem(mp, 2)
    twin_across = lax.rem(twin + 2, 4)

    load_w = pltpu.make_async_copy(w_hbm, w, w_sem)
    load_w.start()
    barrier = pltpu.get_barrier_semaphore()
    for other in (right, left, {"mp": across}, {"mp": twin}):
        pl.semaphore_signal(barrier, inc=1, device_id=other, device_id_type=MESH)

    def greet(k, carry):
        other = {"shard": lax.rem(s + k, owners)}
        pl.semaphore_signal(barrier, inc=1, device_id=other, device_id_type=MESH)
        return carry

    lax.fori_loop(1, owners, greet, 0)

    own = pl.multiple_of(g * span + mp * rows, rows)
    load_w.wait()
    hidden = jnp.dot(states[...], w[...], preferred_element_type=jnp.float32) + bias[...]
    centred = hidden - jnp.mean(hidden, axis=-1, keepdims=True)
    spread = jnp.mean(centred * centred, axis=-1, keepdims=True)
    slab[pl.ds(own, rows), :] = (centred * lax.rsqrt(spread + 1e-05) * gain[...]).astype(jnp.bfloat16)
    q_own = pl.ds(pl.multiple_of(s * 2 * queries, 2 * queries), 2 * queries)
    d_own = pl.ds(pl.multiple_of(s * 8, 8), 8)
    qbuf[q_own, :] = query[...]
    idbuf[d_own, :] = ids[...]
    pl.semaphore_wait(barrier, owners + 3)

    def send(src, dst, send_sem, recv_sem, other):
        return pltpu.make_async_remote_copy(
            src_ref=src, dst_ref=dst, send_sem=send_sem, recv_sem=recv_sem,
            device_id=other, device_id_type=MESH,
        )

    def chunk(ring, lane, part_of):
        return slab.at[pl.ds(pl.multiple_of(ring * span + lane * rows + part_of * half, half), half), :]

    def origin(way, k):
        return lax.rem(g + (rings - k if way == 0 else k), rings)

    def y_copy(stream, way, k, ring):
        c = chunk(ring, across if stream == 2 else mp, 0 if stream == 0 else 1)
        sem = (stream * 2 + way) * 4 + k - 1
        return send(c, c, ys.at[sem], yr.at[sem], right if way == 0 else left)

    def z_copy(ring, lane, part_of):
        c = chunk(ring, lane, part_of)
        sem = ring if part_of == 0 else rings
        return send(c, c, zs.at[sem], zr.at[sem], {"mp": across})

    def c_copy(ring, lane, part_of):
        c = chunk(ring, lane, part_of)
        sem = ring * 4 + lane // 2 * 2 + part_of
        return send(c, c, cs.at[sem], cr.at[sem], {"mp": twin})

    z_copy(g, mp, 1).start()
    for stream in (1, 0):
        for way in (0, 1):
            y_copy(stream, way, 1, g).start()
    z_copy(g, mp, 0).start()
    c_copy(g, mp, 0).start()
    c_copy(g, mp, 1).start()

    def q_copy(p, at):
        there = pl.ds(pl.multiple_of(at * 2 * queries, 2 * queries), 2 * queries)
        return send(query, qbuf.at[there, :], qs.at[p], qr.at[at], {"shard": p})

    def d_copy(p, at):
        there = pl.ds(pl.multiple_of(at * 8, 8), 8)
        return send(ids, idbuf.at[there, :], ds.at[p], dr.at[at], {"shard": p})

    def share(k, carry):
        p = lax.rem(s + k, owners)
        d_copy(p, s).start()
        q_copy(p, s).start()
        return carry

    lax.fori_loop(1, owners, share, 0)

    z_copy(g, across, 1).wait_recv()
    for way in (0, 1):
        y_copy(2, way, 1, g).start()
    c_copy(g, across, 1).start()
    z_copy(g, across, 0).wait_recv()
    c_copy(g, across, 0).start()

    def y_step(k):
        for stream in (2, 1, 0):
            for way in (0, 1):
                if k > REACH[stream][way]:
                    continue
                ring = origin(way, k)
                y_copy(stream, way, k, ring).wait_recv()
                if k < REACH[stream][way]:
                    y_copy(stream, way, k + 1, ring).start()
                if stream == 0:
                    z_copy(ring, mp, 0).start()
                c_copy(ring, across if stream == 2 else mp, 0 if stream == 0 else 1).start()

    def z_step(k):
        for way in (0, 1):
            if k <= REACH[0][way]:
                ring = origin(way, k)
                z_copy(ring, across, 0).wait_recv()
                c_copy(ring, across, 0).start()

    def await_ids(k, carry):
        p = lax.rem(s + k, owners)
        d_copy(p, p).wait_recv()
        return carry

    def await_queries(k, carry):
        p = lax.rem(s + k, owners)
        q_copy(p, p).wait_recv()
        return carry

    def multiplicity(j, carry):
        packed = idbuf[pl.ds(pl.multiple_of(j * 8, 8), 8), :]
        sub = lax.broadcasted_iota(jnp.int32, (128, 128), 0)
        total = jnp.zeros((128, 128), jnp.float32)
        for t in range(5):
            row = packed[t : t + 1, :]
            key = ((row & 0xFFFFF) >> 7) - s * 128
            value = jnp.where((row >> 20) > 0, 129.0, 1.0)
            left_hot = jnp.where(sub == key, value, 0.0).astype(jnp.bfloat16)
            right_hot = jnp.where(sub == (row & 127), 1.0, 0.0).astype(jnp.bfloat16)
            total += lax.dot_general(left_hot, right_hot, NT, preferred_element_type=jnp.float32)
        for hi in range(16):
            cnt[pl.ds(pl.multiple_of(j * 8, 8), 8), hi * 128 : hi * 128 + 128] = total[hi * 8 : hi * 8 + 8, :]
        return carry

    def scores(ring):
        at = pl.ds(pl.multiple_of(ring * span, span), span)
        score[:, at] = lax.dot_general(qmat[...], slab[at, :], NT, preferred_element_type=jnp.float32) * scaling

    def block(k):
        for ring in {0: (g,), 4: (origin(1, 4),)}.get(k, (origin(0, k), origin(1, k))):
            for lane in (twin, twin_across):
                for part_of in (0, 1):
                    c_copy(ring, lane, part_of).wait_recv()
            scores(ring)

    lax.fori_loop(1, owners, await_ids, 0)
    y_step(1)
    lax.fori_loop(0, owners // 2, multiplicity, 0)
    y_step(2)
    z_step(1)
    lax.fori_loop(owners // 2, owners, multiplicity, 0)
    y_step(3)
    z_step(2)
    lax.fori_loop(1, owners, await_queries, 0)
    wide = qbuf[...].astype(jnp.float32).reshape(owners, 2, queries, half_width)
    qmat[:, :half_width] = wide[:, 0].reshape(owners * queries, half_width).astype(jnp.bfloat16)
    qmat[:, half_width:] = wide[:, 1].reshape(owners * queries, half_width).astype(jnp.bfloat16)
    block(0)
    block(1)
    y_step(4)
    z_step(3)
    block(2)
    z_step(4)
    block(3)
    block(4)

    def softmax(j, carry):
        at = pl.ds(pl.multiple_of(j * 16, 16), 16)
        c = cnt[at, :]
        x = score[at, :]
        positive = c >= 128.0
        times = jnp.where(positive, c - 128.0, c)
        x_in = jnp.where(times > 0.0, x, LOW)
        top = jnp.max(x_in, axis=1, keepdims=True)
        e = times * jnp.exp(x_in - top)
        total = jnp.sum(e, axis=1, keepdims=True)
        first = jnp.sum(jnp.where(positive, x, 0.0), axis=1, keepdims=True)
        score[at, :] = e
        lane = lax.broadcasted_iota(jnp.int32, (16, 128), 1)
        stat[at, :] = jnp.where(lane == 0, top, jnp.where(lane == 1, total, jnp.where(lane == 2, first, 0.0)))
        return carry

    lax.fori_loop(0, owners * queries // 16, softmax, 0)
    mine = jnp.transpose(stat[...])[:8, :]
    stats[d_own, :] = mine

    def t_copy(p, at):
        there = stats.at[pl.ds(pl.multiple_of(at * 8, 8), 8), :]
        return send(there, there, ts.at[p], tr.at[at], {"shard": p})

    def tell(k, carry):
        t_copy(lax.rem(s + k, owners), s).start()
        return carry

    def told(k, carry):
        p = lax.rem(s + k, owners)
        t_copy(p, p).wait_recv()
        return carry

    lax.fori_loop(1, owners, tell, 0)
    lax.fori_loop(1, owners, told, 0)
    every = stats[...].reshape(owners, 8, owners * queries)
    top = jnp.max(every, axis=0)[0:1, :]
    share_of = jnp.exp(every[:, 0:1, :] - top.reshape(1, 1, owners * queries))
    total = jnp.sum(every * share_of, axis=0)[1:2, :]
    first = jnp.sum(every, axis=0)[2:3, :]
    factor = jnp.exp(mine[0:1, :] - top) / total
    loss = top + jnp.log(total) - first
    line = lax.broadcasted_iota(jnp.int32, (128, owners * queries), 0)
    back[...] = jnp.transpose(jnp.where(line == 0, factor, jnp.where(line == 1, loss, 0.0)))
    stat_out[...] = back[d_own, :]

    def chances(j, carry):
        at = pl.ds(pl.multiple_of(j * 16, 16), 16)
        positive = jnp.where(cnt[at, :] >= 128.0, 1.0, 0.0)
        prob[at, :] = (score[at, :] * back[at, 0:1] - positive).astype(jnp.bfloat16)
        return carry

    lax.fori_loop(0, owners * queries // 16, chances, 0)

    def p_copy(p, frm, at):
        src = part.at[pl.ds(pl.multiple_of(frm * 2 * queries, 2 * queries), 2 * queries), :]
        there = parts.at[pl.ds(pl.multiple_of(at * 2 * queries, 2 * queries), 2 * queries), :]
        return send(src, there, ps.at[p], pr.at[at], {"shard": p})

    batch = owners // 4

    def gradients(i, carry):
        b = lax.rem(s // batch + i, 4)
        take = pl.ds(pl.multiple_of(b * batch * queries, batch * queries), batch * queries)
        grad = jnp.dot(prob[take, :], slab[...], preferred_element_type=jnp.float32) * scaling
        lo = grad[:, :half_width].reshape(batch, queries, half_width)
        hi = grad[:, half_width:].reshape(batch, queries, half_width)
        both = jnp.concatenate([lo, hi], axis=1).reshape(batch * 2 * queries, half_width)
        put = pl.ds(pl.multiple_of(b * batch * 2 * queries, batch * 2 * queries), batch * 2 * queries)
        part[put, :] = both.astype(jnp.bfloat16)

        def give(k, inner):
            p = b * batch + lax.rem(s + k, batch)

            @pl.when(p != s)
            def _():
                p_copy(p, p, s).start()

            return inner

        lax.fori_loop(0, batch, give, 0)
        return carry

    lax.fori_loop(0, 4, gradients, 0)
    parts[q_own, :] = part[q_own, :]

    def taken(k, carry):
        p = lax.rem(s + k, owners)
        p_copy(p, p, p).wait_recv()
        return carry

    lax.fori_loop(1, owners, taken, 0)
    summed = jnp.sum(parts[...].astype(jnp.float32).reshape(owners, 2 * queries, half_width), axis=0)
    grad_out[:, :half_width] = summed[:queries, :]
    grad_out[:, half_width:] = summed[queries:, :]

    def sent(k, carry):
        p = lax.rem(s + k, owners)
        q_copy(p, s).wait_send()
        d_copy(p, s).wait_send()
        t_copy(p, s).wait_send()
        p_copy(p, p, s).wait_send()
        return carry

    lax.fori_loop(1, owners, sent, 0)
    for stream in range(3):
        for way in (0, 1):
            for k in range(1, REACH[stream][way] + 1):
                y_copy(stream, way, k, origin(way, k - 1)).wait_send()

    def sent_across(ring, carry):
        z_copy(ring, mp, 0).wait_send()
        for lane in (mp, across):
            for part_of in (0, 1):
                c_copy(ring, lane, part_of).wait_send()
        return carry

    lax.fori_loop(0, rings, sent_across, 0)
    z_copy(g, mp, 1).wait_send()


def local(passage_states, query_emb, head_weight, head_bias, norm_gain, candidate_ids):
    rings, owners, parts = lax.axis_size("group"), lax.axis_size("shard"), lax.axis_size("mp")
    rows, width = passage_states.shape
    queries, cands = candidate_ids.shape
    span = parts * rows
    slab_rows = rings * span
    all_queries = owners * queries

    owner = candidate_ids // span % owners
    slab_index = candidate_ids // (span * owners) * span + candidate_ids % span
    line = lax.broadcasted_iota(jnp.int32, candidate_ids.shape, 0)
    column = lax.broadcasted_iota(jnp.int32, candidate_ids.shape, 1)
    key = slab_index // 128 * queries + line
    packed = (column == 0).astype(jnp.int32) * 2**20 + owner * 2**14 + key * 128 + slab_index % 128
    packed = jnp.pad(packed.reshape(-1), (0, 1024 - queries * cands), constant_values=63 * 2**14).reshape(8, 128)
    query = query_emb.reshape(queries, 2, width // 2).transpose(1, 0, 2).reshape(2 * queries, width // 2)

    vmem = pl.BlockSpec(memory_space=pltpu.VMEM)
    dma = pltpu.SemaphoreType.DMA
    bf16, f32 = jnp.bfloat16, jnp.float32
    stat, grad = pl.pallas_call(
        functools.partial(kernel, rings, owners, rows, queries),
        out_shape=(jax.ShapeDtypeStruct((queries, 128), f32), jax.ShapeDtypeStruct((queries, width), f32)),
        in_specs=[vmem] * 5 + [pl.BlockSpec(memory_space=pl.ANY)],
        out_specs=(vmem, vmem),
        scratch_shapes=[
            pltpu.VMEM((width, width), bf16),
            pltpu.VMEM((slab_rows, width), bf16),
            pltpu.VMEM((2 * all_queries, width // 2), bf16),
            pltpu.VMEM((all_queries, width), bf16),
            pltpu.VMEM((owners * 8, 128), jnp.int32),
            pltpu.VMEM((all_queries, slab_rows), f32),
            pltpu.VMEM((all_queries, slab_rows), f32),
            pltpu.VMEM((all_queries, slab_rows), bf16),
            pltpu.VMEM((2 * all_queries, width // 2), bf16),
            pltpu.VMEM((2 * all_queries, width // 2), bf16),
            pltpu.VMEM((all_queries, 128), f32),
            pltpu.VMEM((owners * 8, all_queries), f32),
            pltpu.VMEM((all_queries, 128), f32),
            dma,
            dma((24,)), dma((24,)),
            dma((rings + 1,)), dma((rings + 1,)),
            dma((rings * 4,)), dma((rings * 4,)),
            dma((owners,)), dma((owners,)),
            dma((owners,)), dma((owners,)),
            dma((owners,)), dma((owners,)),
            dma((owners,)), dma((owners,)),
        ],
        compiler_params=pltpu.CompilerParams(
            collective_id=0, has_side_effects=True, vmem_limit_bytes=40 * 2**20
        ),
    )(
        passage_states, query, packed, head_bias.reshape(1, width), norm_gain.reshape(1, width), head_weight,
    )
    return stat[:, 1], grad


def solution(mesh):
    split = P(("group", "shard", "mp"), None)
    in_specs = (split, split, P(), P(), P(), split)
    out_specs = (P(("group", "shard", "mp")), split)
    return jax.shard_map(local, mesh=mesh, in_specs=in_specs, out_specs=out_specs, check_vma=False)
```

```python
import functools
import math

import jax
import jax.numpy as jnp
from jax import lax
from jax.experimental import pallas as pl
from jax.experimental.pallas import tpu as pltpu
from jax.sharding import PartitionSpec as P

MESH = pl.DeviceIdType.MESH
NT = (((1,), (1,)), ((), ()))
LOW = -1e30
F32, BF16 = jnp.float32, jnp.bfloat16


def kernel(
    owners, rows, queries, cands,
    states_in, query_in, w_in, bias_in, gain_in, ids_in,
    loss_out, grad_out,
    states, query, w, bias, gain, raw_ids, query_half, ids,
    slab, qbuf, qmat, idbuf, cnt, score, prob, first, part, parts, stat, stats,
    load_sems, us, ur, ns, nr, vs, vr, cs, cr, qs, qr, ds, dr, ts, tr, ps, pr,
):
    width = w.shape[0]
    half_width = width // 2
    half = rows // 2
    span = 4 * rows
    every = owners * queries
    two = 2 * queries
    scaling = 1.0 / math.sqrt(width)
    y, s, mp = lax.axis_index("group"), lax.axis_index("shard"), lax.axis_index("mp")
    x, z = s // 4, lax.rem(s, 4) * 2 + mp // 2
    core, y_lo = lax.rem(mp, 2), lax.rem(y, 2)
    me = x * 4 + y // 2
    lane = y_lo * 2 + core
    lane_across = lax.rem(lane + 2, 4)
    lane_twin = lane + 1 - 2 * core
    lane_twin_across = lax.rem(lane_twin + 2, 4)

    def at_z(level):
        return {"shard": x * 4 + level // 2, "mp": lax.rem(level, 2) * 2 + core}

    above, below = at_z(lax.rem(z + 1, 8)), at_z(lax.rem(z + 7, 8))
    across = {"group": y + 1 - 2 * y_lo}
    twin = {"mp": mp + 1 - 2 * core}

    def peer(p):
        return {"group": lax.rem(p, 4) * 2 + y_lo, "shard": p // 4 * 4 + s - x * 4}

    def other(k):
        return lax.rem(me + k, owners)

    loads = [
        pltpu.make_async_copy(src, dst, load_sems.at[i])
        for i, (src, dst) in enumerate(
            ((w_in, w), (states_in, states), (bias_in, bias), (gain_in, gain), (query_in, query), (ids_in, raw_ids))
        )
    ]
    for load in loads:
        load.start()

    barrier = pltpu.get_barrier_semaphore()

    def greet(device):
        pl.semaphore_signal(barrier, inc=1, device_id=device, device_id_type=MESH)

    greet(below)

    @pl.when(z < 7)
    def _():
        greet(above)

    greet(across)
    greet(twin)

    def greet_peer(k, carry):
        greet(peer(other(k)))
        return carry

    lax.fori_loop(1, owners, greet_peer, 0)

    for load in loads:
        load.wait()
    hidden = jnp.dot(states[...], w[...], preferred_element_type=F32) + bias[...].reshape(1, width)
    centred = hidden - jnp.mean(hidden, axis=-1, keepdims=True)
    spread = jnp.mean(centred * centred, axis=-1, keepdims=True)
    normal = centred * lax.rsqrt(spread + 1e-05) * gain[...].reshape(1, width)
    slab[pl.ds(pl.multiple_of(z * span + lane * rows, rows), rows), :] = normal.astype(BF16)
    pl.semaphore_wait(barrier, owners + 2 + (z > 0).astype(jnp.int32))

    def send(src, dst, send_sem, recv_sem, device):
        return pltpu.make_async_remote_copy(
            src_ref=src, dst_ref=dst, send_sem=send_sem, recv_sem=recv_sem, device_id=device, device_id_type=MESH,
        )

    def chunk(level, which, h):
        return slab.at[pl.ds(pl.multiple_of(level * span + which * rows + h * half, half), half), :]

    def up(level, h):
        c, sem = chunk(level, lane, h), level * 2 + h
        return send(c, c, us.at[sem], ur.at[sem], above)

    def down(level, h):
        c, sem = chunk(level, lane, h), level * 2 + h
        return send(c, c, ns.at[sem], nr.at[sem], below)

    def over(level, h, which):
        c, sem = chunk(level, which, h), level * 2 + h
        return send(c, c, vs.at[sem], vr.at[sem], across)

    def to_twin(level, h, which):
        c, sem = chunk(level, which, h), level * 4 + which // 2 * 2 + h
        return send(c, c, cs.at[sem], cr.at[sem], twin)

    def reach_up(level):
        return jnp.where(level >= 6, 3, 7 - level)

    def reach_down(level):
        return jnp.where(level >= 6, 4, level)

    for h in (0, 1):
        up(z, h).start()

        @pl.when(z > 0)
        def _(h=h):
            down(z, h).start()

    for h in (0, 1):
        over(z, h, lane).start()
        to_twin(z, h, lane).start()

    wide = query[...].astype(F32)
    query_half[...] = jnp.concatenate([wide[:, :half_width], wide[:, half_width:]], axis=0).astype(BF16)
    raw = raw_ids[...]
    line = lax.broadcasted_iota(jnp.int32, raw.shape, 0)
    column = lax.broadcasted_iota(jnp.int32, raw.shape, 1)
    ring_of = (raw >> 8) & 31
    y_of = raw >> 13
    z_of = (ring_of & 3) * 2 + ((raw >> 7) & 1)
    owner_of = (ring_of >> 2) * 4 + (y_of >> 1)
    key_of = (z_of * 2 + (y_of & 1)) * queries + line
    packed = jnp.where(column == 0, 2**20, 0) + owner_of * 2**14 + key_of * 2**7 + (raw & 127)
    ids[...] = jnp.full(ids.shape, 63 * 2**14, jnp.int32)
    ids[:, :cands] = packed

    def q_at(p):
        return pl.ds(pl.multiple_of(p * two, two), two)

    def d_at(p):
        return pl.ds(pl.multiple_of(p * 8, 8), 8)

    def q_copy(p, at):
        return send(query_half, qbuf.at[q_at(at), :], qs.at[p], qr.at[at], peer(p))

    def d_copy(p, at):
        return send(ids, idbuf.at[d_at(at), :], ds.at[p], dr.at[at], peer(p))

    def share(k, carry):
        d_copy(other(k), me).start()
        q_copy(other(k), me).start()
        return carry

    lax.fori_loop(1, owners, share, 0)
    qbuf[q_at(me), :] = query_half[...]
    idbuf[d_at(me), :] = ids[...]

    def await_share(k, carry):
        p = other(k)
        d_copy(p, p).wait_recv()
        q_copy(p, p).wait_recv()
        return carry

    def multiplicity(j, carry):
        block = idbuf[d_at(j), :]
        sub = lax.broadcasted_iota(jnp.int32, (128, 128), 0)
        total = jnp.zeros((128, 128), F32)
        for t in range(queries):
            row = block[t : t + 1, :]
            key = ((row & 0xFFFFF) >> 7) - me * 128
            value = jnp.where((row >> 20) > 0, 129.0, 1.0)
            left_hot = jnp.where(sub == key, value, 0.0).astype(BF16)
            right_hot = jnp.where(sub == (row & 127), 1.0, 0.0).astype(BF16)
            total += lax.dot_general(left_hot, right_hot, NT, preferred_element_type=F32)
        for hi in range(16):
            cnt[d_at(j), hi * 128 : hi * 128 + 128] = total[hi * 8 : hi * 8 + 8, :]
        return carry

    def rise(k, when):
        level = lax.rem(z - k + 16, 8)
        return when, level, k + 1 <= reach_up(level), up

    def fall(k):
        level = lax.rem(z + k, 8)
        return jnp.logical_and(z + k <= 7, k <= reach_down(level)), level, k + 1 <= reach_down(level), down

    arrivals = []
    for k in range(1, 8):
        arrivals.append(rise(k, z >= k))
        if k <= 5:
            arrivals.append(fall(k))
        if k == 3:
            arrivals.append(rise(z + 1, z <= 2))
        if k == 4:
            arrivals.append(rise(z + 2, z <= 1))

    def arrive(event):
        when, level, goes_on, way = event

        @pl.when(when)
        def _():
            for h in (0, 1):
                way(level, h).wait_recv()

                @pl.when(goes_on)
                def _(h=h):
                    way(level, h).start()

                over(level, h, lane).start()
                to_twin(level, h, lane).start()

    def pass_on(level):
        for h in (0, 1):
            over(level, h, lane_across).wait_recv()
            to_twin(level, h, lane_across).start()

    def use(level):
        for which in (lane_twin, lane_twin_across):
            for h in (0, 1):
                to_twin(level, h, which).wait_recv()
        at = pl.ds(pl.multiple_of(level * span, span), span)
        score[:, at] = lax.dot_general(qmat[...], slab[at, :], NT, preferred_element_type=F32) * scaling

    def later(event, do):
        @pl.when(event[0])
        def _():
            do(event[1])

    pass_on(z)
    for event in arrivals[:4]:
        arrive(event)
    for event in arrivals[:3]:
        later(event, pass_on)
    lax.fori_loop(1, owners, await_share, 0)
    lax.fori_loop(0, owners, multiplicity, 0)
    halves = qbuf[...].astype(F32).reshape(owners, 2, queries, half_width)
    qmat[:, :half_width] = halves[:, 0].reshape(every, half_width).astype(BF16)
    qmat[:, half_width:] = halves[:, 1].reshape(every, half_width).astype(BF16)
    use(z)
    later(arrivals[0], use)
    later(arrivals[1], use)
    for i in range(4, len(arrivals)):
        arrive(arrivals[i])
        later(arrivals[i - 1], pass_on)
        later(arrivals[i - 2], use)
    later(arrivals[-1], pass_on)
    later(arrivals[-2], use)
    later(arrivals[-1], use)

    def softmax(i, carry):
        at = pl.ds(pl.multiple_of(i * 16, 16), 16)
        c = cnt[at, :]
        v = score[at, :]
        positive = c >= 128.0
        times = jnp.where(positive, c - 128.0, c)
        inside = jnp.where(times > 0.0, v, LOW)
        top = jnp.max(inside, axis=1, keepdims=True)
        e = times * jnp.exp(inside - top)
        total = jnp.sum(e, axis=1, keepdims=True)
        named = jnp.sum(jnp.where(positive, v, 0.0), axis=1, keepdims=True)
        prob[at, :] = e.astype(BF16)
        first[at, :] = jnp.where(positive, 1.0, 0.0).astype(BF16)
        spot = lax.broadcasted_iota(jnp.int32, (16, 128), 1) - 4 * (lax.broadcasted_iota(jnp.int32, (16, 128), 0) & 7)
        tile = jnp.where(spot == 0, top, jnp.where(spot == 1, total, jnp.where(spot == 2, named, 0.0)))
        stat[pl.ds(i * 2, 2), :, :] = jnp.sum(tile.reshape(2, 8, 128), axis=1, keepdims=True)
        return carry

    lax.fori_loop(0, every // 16, softmax, 0)

    def t_copy(p, at):
        return send(stat.at[p], stats.at[at], ts.at[p], tr.at[at], peer(p))

    def tell(k, carry):
        t_copy(other(k), me).start()
        return carry

    lax.fori_loop(1, owners, tell, 0)
    stats[pl.ds(me, 1), :, :] = stat[pl.ds(me, 1), :, :]

    def p_at(p):
        return pl.ds(pl.multiple_of(p * 2 * two, 2 * two), 2 * two)

    def p_copy(p, frm, at):
        return send(part.at[p_at(frm), :], parts.at[p_at(at), :], ps.at[p], pr.at[at], peer(p))

    batch = owners // 4

    def partials(i, carry):
        b = lax.rem(me // batch + 2 + i, 4)
        take = pl.ds(pl.multiple_of(b * batch * queries, batch * queries), batch * queries)
        pieces = []
        for weights in (prob, first):
            sums = jnp.dot(weights[take, :], slab[...], preferred_element_type=F32)
            pieces.append(sums[:, :half_width].reshape(batch, queries, half_width))
            pieces.append(sums[:, half_width:].reshape(batch, queries, half_width))
        put = pl.ds(pl.multiple_of(b * batch * 2 * two, batch * 2 * two), batch * 2 * two)
        part[put, :] = jnp.concatenate(pieces, axis=1).reshape(batch * 2 * two, half_width).astype(BF16)

        def give(k, inner):
            p = b * batch + lax.rem(me + k, batch)

            @pl.when(p != me)
            def _():
                p_copy(p, p, me).start()

            return inner

        lax.fori_loop(0, batch, give, 0)
        return carry

    lax.fori_loop(0, 4, partials, 0)
    parts[p_at(me), :] = part[p_at(me), :]

    def told(k, carry):
        t_copy(other(k), other(k)).wait_recv()
        return carry

    lax.fori_loop(1, owners, told, 0)
    told_all = stats[...].reshape(owners, 128)
    top = jnp.max(told_all, axis=0, keepdims=True)
    fade = jnp.exp(jnp.minimum(told_all - top, 0.0))
    total = jnp.sum(pltpu.roll(told_all, 127, 1) * fade, axis=0, keepdims=True)
    named = jnp.sum(pltpu.roll(told_all, 126, 1), axis=0, keepdims=True)
    own_spot = lax.broadcasted_iota(jnp.int32, (1, queries, 128), 2) == 4 * lax.broadcasted_iota(
        jnp.int32, (1, queries, 128), 1
    )

    def upright(flat):
        return jnp.sum(jnp.where(own_spot, flat.reshape(-1, 1, 128), 0.0), axis=2, keepdims=True)

    factor = upright(fade / total)
    loss_out[...] = jnp.broadcast_to(upright(top + jnp.log(total) - named)[0], (queries, 128))

    def taken(k, carry):
        p = other(k)
        p_copy(p, p, p).wait_recv()
        return carry

    lax.fori_loop(1, owners, taken, 0)
    got = parts[...].astype(F32).reshape(owners, 4, queries, half_width)
    for i in (0, 1):
        mean_row = jnp.sum(got[:, i] * factor, axis=0)
        grad_out[:, i * half_width : (i + 1) * half_width] = (mean_row - jnp.sum(got[:, 2 + i], axis=0)) * scaling

    def sent(k, carry):
        p = other(k)
        q_copy(p, me).wait_send()
        d_copy(p, me).wait_send()
        t_copy(p, me).wait_send()
        p_copy(p, p, me).wait_send()
        return carry

    lax.fori_loop(1, owners, sent, 0)

    def sent_rows(level, carry):
        risen, fallen = lax.rem(z - level + 8, 8), level - z

        @pl.when(risen + 1 <= reach_up(level))
        def _():
            for h in (0, 1):
                up(level, h).wait_send()

        @pl.when(jnp.logical_and(fallen >= 0, fallen + 1 <= reach_down(level)))
        def _():
            for h in (0, 1):
                down(level, h).wait_send()

        for h in (0, 1):
            over(level, h, lane).wait_send()
            to_twin(level, h, lane).wait_send()
            to_twin(level, h, lane_across).wait_send()
        return carry

    lax.fori_loop(0, 8, sent_rows, 0)


def local(passage_states, query_emb, head_weight, head_bias, norm_gain, candidate_ids):
    owners = lax.axis_size("shard")
    rows, width = passage_states.shape
    queries, cands = candidate_ids.shape
    slab_rows = 8 * 4 * rows
    every = owners * queries
    dma = pltpu.SemaphoreType.DMA
    vmem = pl.BlockSpec(memory_space=pltpu.VMEM)
    hbm = pl.BlockSpec(memory_space=pltpu.HBM)
    loss, grad = pl.pallas_call(
        functools.partial(kernel, owners, rows, queries, cands),
        out_shape=(jax.ShapeDtypeStruct((queries, 128), F32), jax.ShapeDtypeStruct((queries, width), F32)),
        in_specs=[hbm] * 6,
        out_specs=(vmem, vmem),
        scratch_shapes=[
            pltpu.VMEM((rows, width), BF16),
            pltpu.VMEM((queries, width), BF16),
            pltpu.VMEM((width, width), BF16),
            pltpu.VMEM((width,), F32),
            pltpu.VMEM((width,), F32),
            pltpu.VMEM((queries, cands), jnp.int32),
            pltpu.VMEM((2 * queries, width // 2), BF16),
            pltpu.VMEM((8, 128), jnp.int32),
            pltpu.VMEM((slab_rows, width), BF16),
            pltpu.VMEM((2 * every, width // 2), BF16),
            pltpu.VMEM((every, width), BF16),
            pltpu.VMEM((owners * 8, 128), jnp.int32),
            pltpu.VMEM((every, slab_rows), F32),
            pltpu.VMEM((every, slab_rows), F32),
            pltpu.VMEM((every, slab_rows), BF16),
            pltpu.VMEM((every, slab_rows), BF16),
            pltpu.VMEM((4 * every, width // 2), BF16),
            pltpu.VMEM((4 * every, width // 2), BF16),
            pltpu.VMEM((owners, 1, 128), F32),
            pltpu.VMEM((owners, 1, 128), F32),
            dma((6,)),
            dma((16,)), dma((16,)),
            dma((16,)), dma((16,)),
            dma((16,)), dma((16,)),
            dma((32,)), dma((32,)),
            dma((owners,)), dma((owners,)),
            dma((owners,)), dma((owners,)),
            dma((owners,)), dma((owners,)),
            dma((owners,)), dma((owners,)),
        ],
        compiler_params=pltpu.CompilerParams(
            collective_id=0, has_side_effects=True, vmem_limit_bytes=48 * 2**20
        ),
    )(passage_states, query_emb, head_weight, head_bias, norm_gain, candidate_ids)
    return loss[:, 0], grad


def solution(mesh):
    split = P(("group", "shard", "mp"), None)
    in_specs = (split, split, P(), P(), P(), split)
    out_specs = (P(("group", "shard", "mp")), split)
    return jax.shard_map(local, mesh=mesh, in_specs=in_specs, out_specs=out_specs, check_vma=False)
```

```python
import functools
import math

import jax
import jax.numpy as jnp
from jax import lax
from jax.experimental import pallas as pl
from jax.experimental.pallas import tpu as pltpu
from jax.sharding import PartitionSpec as P

MESH = pl.DeviceIdType.MESH
NT = (((1,), (1,)), ((), ()))
LOW = -1e30
F32, BF16 = jnp.float32, jnp.bfloat16


def kernel(
    owners, rows, queries, cands,
    states_in, query_in, w_in, bias_in, gain_in, ids_in,
    loss_out, grad_out,
    states, query, w, bias, gain, raw_ids, query_half, ids,
    slab, qbuf, qmat, idbuf, cnt, score, both, part, parts, stat, stats,
    load_sems, us, ur, ns, nr, vs, vr, cs, cr, qs, qr, ds, dr, gs, gr, hs, hr, ts, tr, ps, pr,
):
    width = w.shape[0]
    half_width = width // 2
    half = rows // 2
    span = 4 * rows
    every = owners * queries
    two = 2 * queries
    scaling = 1.0 / math.sqrt(width)
    y, s, mp = lax.axis_index("group"), lax.axis_index("shard"), lax.axis_index("mp")
    x, z_hi = s // 4, lax.rem(s, 4)
    z = z_hi * 2 + mp // 2
    core, y_lo = lax.rem(mp, 2), lax.rem(y, 2)
    y_hi = y // 2
    me = x * 4 + y_hi
    lane = y_lo * 2 + core
    lane_across = lax.rem(lane + 2, 4)
    lane_twin = lane + 1 - 2 * core
    lane_twin_across = lax.rem(lane_twin + 2, 4)

    def at_z(level):
        return {"shard": x * 4 + level // 2, "mp": lax.rem(level, 2) * 2 + core}

    above, below = at_z(lax.rem(z + 1, 8)), at_z(lax.rem(z + 7, 8))
    across = {"group": y + 1 - 2 * y_lo}
    twin = {"mp": mp + 1 - 2 * core}

    def peer(p):
        return {"group": lax.rem(p, 4) * 2 + y_lo, "shard": p // 4 * 4 + z_hi}

    def beside(k):
        return x * 4 + lax.rem(y_hi + k, 4)

    def column_of(k):
        return lax.rem(x + k, 8)

    def other(k):
        return lax.rem(me + k, owners)

    loads = [
        pltpu.make_async_copy(src, dst, load_sems.at[i])
        for i, (src, dst) in enumerate(
            ((w_in, w), (states_in, states), (bias_in, bias), (gain_in, gain), (query_in, query), (ids_in, raw_ids))
        )
    ]
    for load in loads:
        load.start()

    barrier = pltpu.get_barrier_semaphore()

    def greet(device):
        pl.semaphore_signal(barrier, inc=1, device_id=device, device_id_type=MESH)

    greet(below)

    @pl.when(z < 7)
    def _():
        greet(above)

    greet(across)
    greet(twin)

    for k in range(1, 4):
        greet(peer(beside(k)))
    for k in range(1, 8):
        greet(peer(column_of(k) * 4 + y_hi))

    for load in loads:
        load.wait()
    hidden = jnp.dot(states[...], w[...], preferred_element_type=F32) + bias[...].reshape(1, width)
    centred = hidden - jnp.mean(hidden, axis=-1, keepdims=True)
    spread = jnp.mean(centred * centred, axis=-1, keepdims=True)
    normal = centred * lax.rsqrt(spread + 1e-05) * gain[...].reshape(1, width)
    slab[pl.ds(pl.multiple_of(z * span + lane * rows, rows), rows), :] = normal.astype(BF16)
    pl.semaphore_wait(barrier, 13 + (z > 0).astype(jnp.int32))

    def send(src, dst, send_sem, recv_sem, device):
        return pltpu.make_async_remote_copy(
            src_ref=src, dst_ref=dst, send_sem=send_sem, recv_sem=recv_sem, device_id=device, device_id_type=MESH,
        )

    def chunk(level, which, h):
        return slab.at[pl.ds(pl.multiple_of(level * span + which * rows + h * half, half), half), :]

    def up(level, h):
        c, sem = chunk(level, lane, h), level * 2 + h
        return send(c, c, us.at[sem], ur.at[sem], above)

    def down(level, h):
        c, sem = chunk(level, lane, h), level * 2 + h
        return send(c, c, ns.at[sem], nr.at[sem], below)

    def over(level, h, which):
        c, sem = chunk(level, which, h), level * 2 + h
        return send(c, c, vs.at[sem], vr.at[sem], across)

    def to_twin(level, h, which):
        c, sem = chunk(level, which, h), level * 4 + which // 2 * 2 + h
        return send(c, c, cs.at[sem], cr.at[sem], twin)

    def reach_up(level):
        return jnp.where(level >= 4, 3, 7 - level)

    def reach_down(level):
        return jnp.where(level >= 4, 4, level)

    for h in (0, 1):
        up(z, h).start()

        @pl.when(z > 0)
        def _(h=h):
            down(z, h).start()

    for h in (0, 1):
        over(z, h, lane).start()
        to_twin(z, h, lane).start()

    wide = query[...].astype(F32)
    query_half[...] = jnp.concatenate([wide[:, :half_width], wide[:, half_width:]], axis=0).astype(BF16)
    raw = raw_ids[...]
    line = lax.broadcasted_iota(jnp.int32, raw.shape, 0)
    column = lax.broadcasted_iota(jnp.int32, raw.shape, 1)
    ring_of = (raw >> 8) & 31
    y_of = raw >> 13
    z_of = (ring_of & 3) * 2 + ((raw >> 7) & 1)
    owner_of = (ring_of >> 2) * 4 + (y_of >> 1)
    key_of = (z_of * 2 + (y_of & 1)) * queries + line
    packed = jnp.where(column == 0, 2**20, 0) + owner_of * 2**14 + key_of * 2**7 + (raw & 127)
    ids[...] = jnp.full(ids.shape, 63 * 2**14, jnp.int32)
    ids[:, :cands] = packed

    def q_at(p):
        return pl.ds(pl.multiple_of(p * two, two), two)

    def d_at(p):
        return pl.ds(pl.multiple_of(p * 8, 8), 8)

    def q_copy(p, at):
        return send(query_half, qbuf.at[q_at(at), :], qs.at[p], qr.at[at], peer(p))

    def d_copy(p, at):
        return send(ids, idbuf.at[d_at(at), :], ds.at[p], dr.at[at], peer(p))

    def column_copies(column, target):
        q_four = qbuf.at[pl.ds(pl.multiple_of(column * 4 * two, 4 * two), 4 * two), :]
        d_four = idbuf.at[pl.ds(pl.multiple_of(column * 32, 32), 32), :]
        device = peer(target * 4 + y_hi)
        return (
            lambda: send(d_four, d_four, gs.at[target], gr.at[column], device),
            lambda: send(q_four, q_four, hs.at[target], hr.at[column], device),
        )

    def share():
        for k in (2, 1, 3):
            d_copy(beside(k), me).start()
            q_copy(beside(k), me).start()

    def share_column():
        for k in range(1, 4):
            p = beside(k)
            d_copy(p, p).wait_recv()
            q_copy(p, p).wait_recv()
        for which in (0, 1):
            for k in (4, 3, 5, 2, 6, 1, 7):
                column_copies(x, column_of(k))[which]().start()

    def await_columns():
        for k in range(1, 8):
            for copy in column_copies(column_of(k), column_of(k)):
                copy().wait_recv()

    qbuf[q_at(me), :] = query_half[...]
    idbuf[d_at(me), :] = ids[...]

    def multiplicity(j, carry):
        block = idbuf[d_at(j), :]
        sub = lax.broadcasted_iota(jnp.int32, (128, 128), 0)
        left_hot, right_hot = [], []
        for t in range(queries):
            row = block[t : t + 1, :]
            key = ((row & 0xFFFFF) >> 7) - me * 128
            value = jnp.where((row >> 20) > 0, 129.0, 1.0)
            left_hot.append(jnp.where(sub == key, value, 0.0).astype(BF16))
            right_hot.append(jnp.where(sub == (row & 127), 1.0, 0.0).astype(BF16))
        left_hot, right_hot = jnp.concatenate(left_hot, axis=1), jnp.concatenate(right_hot, axis=1)
        total = lax.dot_general(left_hot, right_hot, NT, preferred_element_type=F32)
        for hi in range(16):
            cnt[d_at(j), hi * 128 : hi * 128 + 128] = total[hi * 8 : hi * 8 + 8, :]
        return carry

    def rise(k, when):
        level = lax.rem(z - k + 16, 8)
        return when, level, k + 1 <= reach_up(level), up

    def fall(k):
        level = lax.rem(z + k, 8)
        return jnp.logical_and(z + k <= 7, k <= reach_down(level)), level, k + 1 <= reach_down(level), down

    ups = {k: rise(k, z >= k) for k in range(1, 8)}
    falls = {k: fall(k) for k in range(1, 5)}
    wraps = {k: rise(z + k, z + k <= 3) for k in range(1, 4)}
    arrivals = [
        ups[1], ups[2], falls[1], ups[3], falls[2], ups[4], falls[3],
        wraps[1], wraps[2], falls[4], wraps[3], ups[5], ups[6], ups[7],
    ]

    def arrive(event):
        when, level, goes_on, way = event

        @pl.when(when)
        def _():
            for h in (0, 1):
                way(level, h).wait_recv()

                @pl.when(goes_on)
                def _(h=h):
                    way(level, h).start()

                over(level, h, lane).start()
                to_twin(level, h, lane).start()

    def pass_on(level):
        for h in (0, 1):
            over(level, h, lane_across).wait_recv()
            to_twin(level, h, lane_across).start()

    def use(level):
        for which in (lane_twin, lane_twin_across):
            for h in (0, 1):
                to_twin(level, h, which).wait_recv()
        at = pl.ds(pl.multiple_of(level * span, span), span)
        score[:, at] = lax.dot_general(qmat[...], slab[at, :], NT, preferred_element_type=F32) * scaling

    def later(event, do):
        @pl.when(event[0])
        def _():
            do(event[1])

    arrive(arrivals[0])
    share()

    def prepare():
        await_columns()
        lax.fori_loop(0, owners, multiplicity, 0, unroll=4)
        halves = qbuf[...].astype(F32).reshape(owners, 2, queries, half_width)
        qmat[:, :half_width] = halves[:, 0].reshape(every, half_width).astype(BF16)
        qmat[:, half_width:] = halves[:, 1].reshape(every, half_width).astype(BF16)

    order = [(True, z)] + arrivals
    met = 9
    for i in range(2, len(order)):
        arrive(order[i])
        later(order[i - 2], pass_on)
        if i == 3:
            share_column()
        if i == met:
            prepare()
            for event in order[: met - 3]:
                later(event, use)
        if i > met:
            later(order[i - 4], use)
    for event in order[-2:]:
        later(event, pass_on)
    for event in order[-4:]:
        later(event, use)

    batch = owners // 4
    per_batch = batch * queries // 16

    def softmax(i, carry):
        at = pl.ds(pl.multiple_of(i * 16, 16), 16)
        c = cnt[at, :]
        v = score[at, :]
        positive = c >= 128.0
        times = jnp.where(positive, c - 128.0, c)
        inside = jnp.where(times > 0.0, v, LOW)
        top = jnp.max(inside, axis=1, keepdims=True)
        e = times * jnp.exp(inside - top)
        total = jnp.sum(e, axis=1, keepdims=True)
        named = jnp.sum(jnp.where(positive, v, 0.0), axis=1, keepdims=True)
        put = pl.multiple_of(i // per_batch * 2 * batch * queries + lax.rem(i, per_batch) * 16, 16)
        both[pl.ds(put, 16), :] = e.astype(BF16)
        both[pl.ds(pl.multiple_of(put + batch * queries, 16), 16), :] = jnp.where(positive, 1.0, 0.0).astype(BF16)
        spot = lax.broadcasted_iota(jnp.int32, (16, 128), 1) - 4 * (lax.broadcasted_iota(jnp.int32, (16, 128), 0) & 7)
        tile = jnp.where(spot == 0, top, jnp.where(spot == 1, total, jnp.where(spot == 2, named, 0.0)))
        stat[pl.ds(i * 2, 2), :, :] = jnp.sum(tile.reshape(2, 8, 128), axis=1, keepdims=True)
        return carry

    lax.fori_loop(0, every // 16, softmax, 0, unroll=4)

    def t_copy(p, at):
        return send(stat.at[p], stats.at[at], ts.at[p], tr.at[at], peer(p))

    def tell(k, carry):
        t_copy(other(k), me).start()
        return carry

    lax.fori_loop(1, owners, tell, 0)
    stats[pl.ds(me, 1), :, :] = stat[pl.ds(me, 1), :, :]

    def p_at(p):
        return pl.ds(pl.multiple_of(p * 2 * two, 2 * two), 2 * two)

    def p_copy(p, frm, at):
        return send(part.at[p_at(frm), :], parts.at[p_at(at), :], ps.at[p], pr.at[at], peer(p))

    def partials(i, carry):
        b = lax.rem(x // 2 + jnp.where(i == 0, 2, jnp.where(i == 1, 1, jnp.where(i == 2, 3, 0))), 4)
        take = pl.ds(pl.multiple_of(b * 2 * batch * queries, 2 * batch * queries), 2 * batch * queries)
        sums = jnp.dot(both[take, :], slab[...], preferred_element_type=F32)
        pieces = [
            sums[i * batch * queries : (i + 1) * batch * queries, j * half_width : (j + 1) * half_width].reshape(
                batch, queries, half_width
            )
            for i in (0, 1)
            for j in (0, 1)
        ]
        put = pl.ds(pl.multiple_of(b * batch * 2 * two, batch * 2 * two), batch * 2 * two)
        part[put, :] = jnp.concatenate(pieces, axis=1).reshape(batch * 2 * two, half_width).astype(BF16)

        def give(pairs):
            def one(k, inner):
                for pair in pairs:
                    p = lax.rem(x // 2 + pair, 4) * batch + lax.rem(k, 2) * 4 + lax.rem(y_hi + 2 + 3 * (k // 2), 4)

                    @pl.when(p != me)
                    def _(p=p):
                        p_copy(p, p, me).start()

                return inner

            lax.fori_loop(0, batch, one, 0)

        for step, pairs in ((0, (2,)), (2, (1, 3)), (3, (0,))):

            @pl.when(i == step)
            def _(pairs=pairs):
                give(pairs)

        return carry

    lax.fori_loop(0, 4, partials, 0)
    parts[p_at(me), :] = part[p_at(me), :]

    def told(k, carry):
        t_copy(other(k), other(k)).wait_recv()
        return carry

    lax.fori_loop(1, owners, told, 0)
    told_all = stats[...].reshape(owners, 128)
    top = jnp.max(told_all, axis=0, keepdims=True)
    fade = jnp.exp(jnp.minimum(told_all - top, 0.0))
    total = jnp.sum(pltpu.roll(told_all, 127, 1) * fade, axis=0, keepdims=True)
    named = jnp.sum(pltpu.roll(told_all, 126, 1), axis=0, keepdims=True)
    own_spot = lax.broadcasted_iota(jnp.int32, (1, queries, 128), 2) == 4 * lax.broadcasted_iota(
        jnp.int32, (1, queries, 128), 1
    )

    def upright(flat):
        return jnp.sum(jnp.where(own_spot, flat.reshape(-1, 1, 128), 0.0), axis=2, keepdims=True)

    factor = upright(fade / total)
    loss_out[...] = jnp.broadcast_to(upright(top + jnp.log(total) - named)[0], (queries, 128))

    def taken(k, carry):
        p = other(k)
        p_copy(p, p, p).wait_recv()
        return carry

    lax.fori_loop(1, owners, taken, 0)
    got = parts[...].astype(F32).reshape(owners, 4, queries, half_width)
    for i in (0, 1):
        mean_row = jnp.sum(got[:, i] * factor, axis=0)
        grad_out[:, i * half_width : (i + 1) * half_width] = (mean_row - jnp.sum(got[:, 2 + i], axis=0)) * scaling

    def sent(k, carry):
        p = other(k)
        t_copy(p, me).wait_send()
        p_copy(p, p, me).wait_send()
        return carry

    lax.fori_loop(1, owners, sent, 0)

    for k in range(1, 4):
        d_copy(beside(k), me).wait_send()
        q_copy(beside(k), me).wait_send()
    for k in range(1, 8):
        for copy in column_copies(x, column_of(k)):
            copy().wait_send()

    def sent_rows(level, carry):
        risen, fallen = lax.rem(z - level + 8, 8), level - z

        @pl.when(risen + 1 <= reach_up(level))
        def _():
            for h in (0, 1):
                up(level, h).wait_send()

        @pl.when(jnp.logical_and(fallen >= 0, fallen + 1 <= reach_down(level)))
        def _():
            for h in (0, 1):
                down(level, h).wait_send()

        for h in (0, 1):
            over(level, h, lane).wait_send()
            to_twin(level, h, lane).wait_send()
            to_twin(level, h, lane_across).wait_send()
        return carry

    lax.fori_loop(0, 8, sent_rows, 0)


def local(passage_states, query_emb, head_weight, head_bias, norm_gain, candidate_ids):
    owners = lax.axis_size("shard")
    rows, width = passage_states.shape
    queries, cands = candidate_ids.shape
    slab_rows = 8 * 4 * rows
    every = owners * queries
    dma = pltpu.SemaphoreType.DMA
    vmem = pl.BlockSpec(memory_space=pltpu.VMEM)
    hbm = pl.BlockSpec(memory_space=pltpu.HBM)
    loss, grad = pl.pallas_call(
        functools.partial(kernel, owners, rows, queries, cands),
        out_shape=(jax.ShapeDtypeStruct((queries, 128), F32), jax.ShapeDtypeStruct((queries, width), F32)),
        in_specs=[hbm] * 6,
        out_specs=(vmem, vmem),
        scratch_shapes=[
            pltpu.VMEM((rows, width), BF16),
            pltpu.VMEM((queries, width), BF16),
            pltpu.VMEM((width, width), BF16),
            pltpu.VMEM((width,), F32),
            pltpu.VMEM((width,), F32),
            pltpu.VMEM((queries, cands), jnp.int32),
            pltpu.VMEM((2 * queries, width // 2), BF16),
            pltpu.VMEM((8, 128), jnp.int32),
            pltpu.VMEM((slab_rows, width), BF16),
            pltpu.VMEM((2 * every, width // 2), BF16),
            pltpu.VMEM((every, width), BF16),
            pltpu.VMEM((owners * 8, 128), jnp.int32),
            pltpu.VMEM((every, slab_rows), F32),
            pltpu.VMEM((every, slab_rows), F32),
            pltpu.VMEM((2 * every, slab_rows), BF16),
            pltpu.VMEM((4 * every, width // 2), BF16),
            pltpu.VMEM((4 * every, width // 2), BF16),
            pltpu.VMEM((owners, 1, 128), F32),
            pltpu.VMEM((owners, 1, 128), F32),
            dma((6,)),
            dma((16,)), dma((16,)),
            dma((16,)), dma((16,)),
            dma((16,)), dma((16,)),
            dma((32,)), dma((32,)),
            dma((owners,)), dma((owners,)),
            dma((owners,)), dma((owners,)),
            dma((8,)), dma((8,)),
            dma((8,)), dma((8,)),
            dma((owners,)), dma((owners,)),
            dma((owners,)), dma((owners,)),
        ],
        compiler_params=pltpu.CompilerParams(
            collective_id=0, has_side_effects=True, vmem_limit_bytes=63 * 2**20
        ),
    )(passage_states, query_emb, head_weight, head_bias, norm_gain, candidate_ids)
    return loss[:, 0], grad


def solution(mesh):
    split = P(("group", "shard", "mp"), None)
    in_specs = (split, split, P(), P(), P(), split)
    out_specs = (P(("group", "shard", "mp")), split)
    return jax.shard_map(local, mesh=mesh, in_specs=in_specs, out_specs=out_specs, check_vma=False)
```

```python
import functools
import math

import jax
import jax.numpy as jnp
from jax import lax
from jax.experimental import pallas as pl
from jax.experimental.pallas import tpu as pltpu
from jax.sharding import PartitionSpec as P

MESH = pl.DeviceIdType.MESH
NT = (((1,), (1,)), ((), ()))
LOW = -1e30
F32, BF16 = jnp.float32, jnp.bfloat16


def kernel(
    owners, rows, queries, cands,
    states_in, query_in, w_in, bias_in, gain_in, ids_in,
    loss_out, grad_out,
    states, query, w, bias, gain, raw_ids, query_half, ids,
    slab, qbuf, qmat, idbuf, cnt, score, both, part, parts, stat, stats,
    load_sems, us, ur, ns, nr, vs, vr, cs, cr, qs, qr, ds, dr, gs, gr, hs, hr, ts, tr, ps, pr,
):
    width = w.shape[0]
    half_width = width // 2
    half = rows // 2
    span = 4 * rows
    every = owners * queries
    two = 2 * queries
    scaling = 1.0 / math.sqrt(width)
    y, s, mp = lax.axis_index("group"), lax.axis_index("shard"), lax.axis_index("mp")
    x, z_hi = s // 4, lax.rem(s, 4)
    z = z_hi * 2 + mp // 2
    core, y_lo = lax.rem(mp, 2), lax.rem(y, 2)
    y_hi = y // 2
    me = x * 4 + y_hi
    lane = y_lo * 2 + core
    lane_across = lax.rem(lane + 2, 4)
    lane_twin = lane + 1 - 2 * core
    lane_twin_across = lax.rem(lane_twin + 2, 4)

    def at_z(level):
        return {"shard": x * 4 + level // 2, "mp": lax.rem(level, 2) * 2 + core}

    above, below = at_z(lax.rem(z + 1, 8)), at_z(lax.rem(z + 7, 8))
    across = {"group": y + 1 - 2 * y_lo}
    twin = {"mp": mp + 1 - 2 * core}

    def peer(p):
        return {"group": lax.rem(p, 4) * 2 + y_lo, "shard": p // 4 * 4 + z_hi}

    def beside(k):
        return x * 4 + lax.rem(y_hi + k, 4)

    def column_of(k):
        return lax.rem(x + k, 8)

    def other(k):
        return lax.rem(me + k, owners)

    loads = [
        pltpu.make_async_copy(src, dst, load_sems.at[i])
        for i, (src, dst) in enumerate(
            ((w_in, w), (states_in, states), (bias_in, bias), (gain_in, gain), (query_in, query), (ids_in, raw_ids))
        )
    ]
    for load in loads:
        load.start()

    barrier = pltpu.get_barrier_semaphore()

    def greet(device):
        pl.semaphore_signal(barrier, inc=1, device_id=device, device_id_type=MESH)

    greet(below)

    @pl.when(z < 7)
    def _():
        greet(above)

    greet(across)
    greet(twin)

    for k in range(1, 4):
        greet(peer(beside(k)))
    for k in range(1, 8):
        greet(peer(column_of(k) * 4 + y_hi))

    for load in loads:
        load.wait()
    hidden = jnp.dot(states[...], w[...], preferred_element_type=F32) + bias[...].reshape(1, width)
    centred = hidden - jnp.mean(hidden, axis=-1, keepdims=True)
    spread = jnp.mean(centred * centred, axis=-1, keepdims=True)
    normal = centred * lax.rsqrt(spread + 1e-05) * gain[...].reshape(1, width)
    slab[pl.ds(pl.multiple_of(z * span + lane * rows, rows), rows), :] = normal.astype(BF16)
    pl.semaphore_wait(barrier, 13 + (z > 0).astype(jnp.int32))

    def send(src, dst, send_sem, recv_sem, device):
        return pltpu.make_async_remote_copy(
            src_ref=src, dst_ref=dst, send_sem=send_sem, recv_sem=recv_sem, device_id=device, device_id_type=MESH,
        )

    def chunk(level, which, h):
        return slab.at[pl.ds(pl.multiple_of(level * span + which * rows + h * half, half), half), :]

    def up(level, h):
        c, sem = chunk(level, lane, h), level * 2 + h
        return send(c, c, us.at[sem], ur.at[sem], above)

    def down(level, h):
        c, sem = chunk(level, lane, h), level * 2 + h
        return send(c, c, ns.at[sem], nr.at[sem], below)

    def over(level, h, which):
        c, sem = chunk(level, which, h), level * 2 + h
        return send(c, c, vs.at[sem], vr.at[sem], across)

    def to_twin(level, h, which):
        c, sem = chunk(level, which, h), level * 4 + which // 2 * 2 + h
        return send(c, c, cs.at[sem], cr.at[sem], twin)

    def reach_up(level):
        return jnp.where(level >= 4, 3, 7 - level)

    def reach_down(level):
        return jnp.where(level >= 4, 4, level)

    for h in (0, 1):
        up(z, h).start()

        @pl.when(z > 0)
        def _(h=h):
            down(z, h).start()

    for h in (0, 1):
        over(z, h, lane).start()
        to_twin(z, h, lane).start()

    wide = query[...].astype(F32)
    query_half[...] = jnp.concatenate([wide[:, :half_width], wide[:, half_width:]], axis=0).astype(BF16)
    raw = raw_ids[...]
    line = lax.broadcasted_iota(jnp.int32, raw.shape, 0)
    column = lax.broadcasted_iota(jnp.int32, raw.shape, 1)
    ring_of = (raw >> 8) & 31
    y_of = raw >> 13
    z_of = (ring_of & 3) * 2 + ((raw >> 7) & 1)
    owner_of = (ring_of >> 2) * 4 + (y_of >> 1)
    key_of = (z_of * 2 + (y_of & 1)) * queries + line
    packed = jnp.where(column == 0, 2**20, 0) + owner_of * 2**14 + key_of * 2**7 + (raw & 127)
    ids[...] = jnp.full(ids.shape, 63 * 2**14, jnp.int32)
    ids[:, :cands] = packed

    def q_at(p):
        return pl.ds(pl.multiple_of(p * two, two), two)

    def d_at(p):
        return pl.ds(pl.multiple_of(p * 8, 8), 8)

    def q_copy(p, at):
        return send(query_half, qbuf.at[q_at(at), :], qs.at[p], qr.at[at], peer(p))

    def d_copy(p, at):
        return send(ids, idbuf.at[d_at(at), :], ds.at[p], dr.at[at], peer(p))

    def column_copies(column, target):
        q_four = qbuf.at[pl.ds(pl.multiple_of(column * 4 * two, 4 * two), 4 * two), :]
        d_four = idbuf.at[pl.ds(pl.multiple_of(column * 32, 32), 32), :]
        device = peer(target * 4 + y_hi)
        return (
            lambda: send(d_four, d_four, gs.at[target], gr.at[column], device),
            lambda: send(q_four, q_four, hs.at[target], hr.at[column], device),
        )

    def share():
        for k in (2, 1, 3):
            d_copy(beside(k), me).start()
            q_copy(beside(k), me).start()

    def share_column():
        for k in range(1, 4):
            p = beside(k)
            d_copy(p, p).wait_recv()
            q_copy(p, p).wait_recv()
        for which in (0, 1):
            for k in (4, 3, 5, 2, 6, 1, 7):
                column_copies(x, column_of(k))[which]().start()

    def await_columns():
        for k in range(1, 8):
            for copy in column_copies(column_of(k), column_of(k)):
                copy().wait_recv()

    qbuf[q_at(me), :] = query_half[...]
    idbuf[d_at(me), :] = ids[...]

    def multiplicity(j, carry):
        block = idbuf[d_at(j), :]
        sub = lax.broadcasted_iota(jnp.int32, (128, 128), 0)
        left_hot, right_hot = [], []
        for t in range(queries):
            row = block[t : t + 1, :]
            key = ((row & 0xFFFFF) >> 7) - me * 128
            value = jnp.where((row >> 20) > 0, 129.0, 1.0)
            left_hot.append(jnp.where(sub == key, value, 0.0).astype(BF16))
            right_hot.append(jnp.where(sub == (row & 127), 1.0, 0.0).astype(BF16))
        left_hot, right_hot = jnp.concatenate(left_hot, axis=1), jnp.concatenate(right_hot, axis=1)
        total = lax.dot_general(left_hot, right_hot, NT, preferred_element_type=F32)
        for hi in range(16):
            cnt[d_at(j), hi * 128 : hi * 128 + 128] = total[hi * 8 : hi * 8 + 8, :]
        return carry

    def rise(k, when):
        level = lax.rem(z - k + 16, 8)
        return when, level, k + 1 <= reach_up(level), up

    def fall(k):
        level = lax.rem(z + k, 8)
        return jnp.logical_and(z + k <= 7, k <= reach_down(level)), level, k + 1 <= reach_down(level), down

    ups = {k: rise(k, z >= k) for k in range(1, 8)}
    falls = {k: fall(k) for k in range(1, 5)}
    wraps = {k: rise(z + k, z + k <= 3) for k in range(1, 4)}
    arrivals = [
        ups[1], ups[2], falls[1], ups[3], falls[2], ups[4], falls[3],
        ups[5], ups[6], ups[7], wraps[1], wraps[2], falls[4], wraps[3],
    ]

    def arrive(event):
        when, level, goes_on, way = event

        @pl.when(when)
        def _():
            for h in (0, 1):
                way(level, h).wait_recv()

                @pl.when(goes_on)
                def _(h=h):
                    way(level, h).start()

                over(level, h, lane).start()
                to_twin(level, h, lane).start()

    def pass_on(level):
        for h in (0, 1):
            over(level, h, lane_across).wait_recv()
            to_twin(level, h, lane_across).start()

    def use(level):
        for which in (lane_twin, lane_twin_across):
            for h in (0, 1):
                to_twin(level, h, which).wait_recv()
        at = pl.ds(pl.multiple_of(level * span, span), span)
        score[:, at] = lax.dot_general(qmat[...], slab[at, :], NT, preferred_element_type=F32) * scaling

    def later(event, do):
        @pl.when(event[0])
        def _():
            do(event[1])

    arrive(arrivals[0])
    share()

    def count(step, steps):
        lax.fori_loop(step * owners // steps, (step + 1) * owners // steps, multiplicity, 0, unroll=4)

    def widen():
        halves = qbuf[...].astype(F32).reshape(owners, 2, queries, half_width)
        qmat[:, :half_width] = halves[:, 0].reshape(every, half_width).astype(BF16)
        qmat[:, half_width:] = halves[:, 1].reshape(every, half_width).astype(BF16)

    order = [(True, z)] + arrivals
    upper, met = z >= 4, 12
    lower = jnp.logical_not(upper)
    for i in range(2, len(order)):
        arrive(order[i])
        if i == 9:
            later((jnp.logical_and(upper, order[7][0]), order[7][1]), pass_on)
        else:
            later(order[i - 2], pass_on)
        if i == 3:
            share_column()
        if 7 <= i <= 10:

            @pl.when(upper)
            def _(i=i):
                if i == 7:
                    await_columns()
                count(i - 7, 4)
                if i == 10:
                    widen()

        if i == 9:

            @pl.when(lower)
            def _():
                await_columns()
                count(0, 2)

        if i == met:
            later((jnp.logical_and(lower, order[7][0]), order[7][1]), pass_on)

            @pl.when(lower)
            def _():
                count(1, 2)
                widen()

            for event in order[: met - 3]:
                later(event, use)
        if i > met:
            later(order[i - 4], use)
    for event in order[-2:]:
        later(event, pass_on)
    for event in order[-4:]:
        later(event, use)

    batch = owners // 4
    per_batch = batch * queries // 16

    def softmax(i, carry):
        at = pl.ds(pl.multiple_of(i * 16, 16), 16)
        c = cnt[at, :]
        v = score[at, :]
        positive = c >= 128.0
        times = jnp.where(positive, c - 128.0, c)
        inside = jnp.where(times > 0.0, v, LOW)
        top = jnp.max(inside, axis=1, keepdims=True)
        e = times * jnp.exp(inside - top)
        total = jnp.sum(e, axis=1, keepdims=True)
        named = jnp.sum(jnp.where(positive, v, 0.0), axis=1, keepdims=True)
        put = pl.multiple_of(i // per_batch * 2 * batch * queries + lax.rem(i, per_batch) * 16, 16)
        both[pl.ds(put, 16), :] = e.astype(BF16)
        both[pl.ds(pl.multiple_of(put + batch * queries, 16), 16), :] = jnp.where(positive, 1.0, 0.0).astype(BF16)
        spot = lax.broadcasted_iota(jnp.int32, (16, 128), 1) - (lax.broadcasted_iota(jnp.int32, (16, 128), 0) & 7)
        tile = jnp.where(spot == 0, top, jnp.where(spot == 8, total, jnp.where(spot == 16, named, 0.0)))
        stat[pl.ds(i * 2, 2), :, :] = jnp.sum(tile.reshape(2, 8, 128), axis=1, keepdims=True)
        return carry

    lax.fori_loop(0, every // 16, softmax, 0, unroll=4)

    def t_copy(p, at):
        return send(stat.at[p], stats.at[at], ts.at[p], tr.at[at], peer(p))

    def tell(k, carry):
        t_copy(other(k), me).start()
        return carry

    lax.fori_loop(1, owners, tell, 0)
    stats[pl.ds(me, 1), :, :] = stat[pl.ds(me, 1), :, :]

    def p_at(p):
        return pl.ds(pl.multiple_of(p * 2 * two, 2 * two), 2 * two)

    def p_copy(p, frm, at):
        return send(part.at[p_at(frm), :], parts.at[p_at(at), :], ps.at[p], pr.at[at], peer(p))

    def partials(i, carry):
        b = lax.rem(x // 2 + jnp.where(i == 0, 2, jnp.where(i == 1, 1, jnp.where(i == 2, 3, 0))), 4)
        take = pl.ds(pl.multiple_of(b * 2 * batch * queries, 2 * batch * queries), 2 * batch * queries)
        sums = jnp.dot(both[take, :], slab[...], preferred_element_type=F32)
        pieces = [
            sums[i * batch * queries : (i + 1) * batch * queries, j * half_width : (j + 1) * half_width].reshape(
                batch, queries, half_width
            )
            for i in (0, 1)
            for j in (0, 1)
        ]
        put = pl.ds(pl.multiple_of(b * batch * 2 * two, batch * 2 * two), batch * 2 * two)
        part[put, :] = jnp.concatenate(pieces, axis=1).reshape(batch * 2 * two, half_width).astype(BF16)

        def give(pairs):
            def one(k, inner):
                for pair in pairs:
                    p = lax.rem(x // 2 + pair, 4) * batch + lax.rem(k, 2) * 4 + lax.rem(y_hi + 2 + 3 * (k // 2), 4)

                    @pl.when(p != me)
                    def _(p=p):
                        p_copy(p, p, me).start()

                return inner

            lax.fori_loop(0, batch, one, 0)

        for step, pairs in ((0, (2,)), (2, (1, 3)), (3, (0,))):

            @pl.when(i == step)
            def _(pairs=pairs):
                give(pairs)

        return carry

    lax.fori_loop(0, 4, partials, 0)
    parts[p_at(me), :] = part[p_at(me), :]

    def told(k, carry):
        t_copy(other(k), other(k)).wait_recv()
        return carry

    lax.fori_loop(1, owners, told, 0)
    told_all = stats[...].reshape(owners, 128)
    top = jnp.max(told_all, axis=0, keepdims=True)
    fade = jnp.exp(jnp.minimum(told_all - top, 0.0))
    total = jnp.sum(pltpu.roll(told_all, 120, 1) * fade, axis=0, keepdims=True)
    named = jnp.sum(pltpu.roll(told_all, 112, 1), axis=0, keepdims=True)
    own_spot = lax.broadcasted_iota(jnp.int32, (1, queries, 128), 2) == lax.broadcasted_iota(
        jnp.int32, (1, queries, 128), 1
    )

    def upright(flat):
        return jnp.sum(jnp.where(own_spot, flat.reshape(-1, 1, 128), 0.0), axis=2, keepdims=True)

    factor = upright(fade / total)
    loss_out[...] = jnp.broadcast_to(top + jnp.log(total) - named, (queries, 128))

    def taken(k, carry):
        p = other(k)
        p_copy(p, p, p).wait_recv()
        return carry

    lax.fori_loop(1, owners, taken, 0)
    got = parts[...].astype(F32).reshape(owners, 4, queries, half_width)
    for i in (0, 1):
        mean_row = jnp.sum(got[:, i] * factor, axis=0)
        grad_out[:, i * half_width : (i + 1) * half_width] = (mean_row - jnp.sum(got[:, 2 + i], axis=0)) * scaling

    def sent(k, carry):
        p = other(k)
        t_copy(p, me).wait_send()
        p_copy(p, p, me).wait_send()
        return carry

    lax.fori_loop(1, owners, sent, 0)

    for k in range(1, 4):
        d_copy(beside(k), me).wait_send()
        q_copy(beside(k), me).wait_send()
    for k in range(1, 8):
        for copy in column_copies(x, column_of(k)):
            copy().wait_send()

    def sent_rows(level, carry):
        risen, fallen = lax.rem(z - level + 8, 8), level - z

        @pl.when(risen + 1 <= reach_up(level))
        def _():
            for h in (0, 1):
                up(level, h).wait_send()

        @pl.when(jnp.logical_and(fallen >= 0, fallen + 1 <= reach_down(level)))
        def _():
            for h in (0, 1):
                down(level, h).wait_send()

        for h in (0, 1):
            over(level, h, lane).wait_send()
            to_twin(level, h, lane).wait_send()
            to_twin(level, h, lane_across).wait_send()
        return carry

    lax.fori_loop(0, 8, sent_rows, 0)


def finish(loss_in, grad_in, loss_out, grad_out, loss, sems):
    copies = [
        pltpu.make_async_copy(loss_in, loss, sems.at[0]),
        pltpu.make_async_copy(grad_in, grad_out, sems.at[1]),
    ]
    for copy in copies:
        copy.start()
    for copy in copies:
        copy.wait()
    loss_out[...] = loss[0, : loss_out.shape[0]]


def local(passage_states, query_emb, head_weight, head_bias, norm_gain, candidate_ids):
    owners = lax.axis_size("shard")
    rows, width = passage_states.shape
    queries, cands = candidate_ids.shape
    slab_rows = 8 * 4 * rows
    every = owners * queries
    dma = pltpu.SemaphoreType.DMA
    vmem = pl.BlockSpec(memory_space=pltpu.VMEM)
    hbm = pl.BlockSpec(memory_space=pltpu.HBM)
    loss, grad = pl.pallas_call(
        functools.partial(kernel, owners, rows, queries, cands),
        out_shape=(jax.ShapeDtypeStruct((queries, 128), F32), jax.ShapeDtypeStruct((queries, width), F32)),
        in_specs=[hbm] * 6,
        out_specs=(vmem, vmem),
        scratch_shapes=[
            pltpu.VMEM((rows, width), BF16),
            pltpu.VMEM((queries, width), BF16),
            pltpu.VMEM((width, width), BF16),
            pltpu.VMEM((width,), F32),
            pltpu.VMEM((width,), F32),
            pltpu.VMEM((queries, cands), jnp.int32),
            pltpu.VMEM((2 * queries, width // 2), BF16),
            pltpu.VMEM((8, 128), jnp.int32),
            pltpu.VMEM((slab_rows, width), BF16),
            pltpu.VMEM((2 * every, width // 2), BF16),
            pltpu.VMEM((every, width), BF16),
            pltpu.VMEM((owners * 8, 128), jnp.int32),
            pltpu.VMEM((every, slab_rows), F32),
            pltpu.VMEM((every, slab_rows), F32),
            pltpu.VMEM((2 * every, slab_rows), BF16),
            pltpu.VMEM((4 * every, width // 2), BF16),
            pltpu.VMEM((4 * every, width // 2), BF16),
            pltpu.VMEM((owners, 1, 128), F32),
            pltpu.VMEM((owners, 1, 128), F32),
            dma((6,)),
            dma((16,)), dma((16,)),
            dma((16,)), dma((16,)),
            dma((16,)), dma((16,)),
            dma((32,)), dma((32,)),
            dma((owners,)), dma((owners,)),
            dma((owners,)), dma((owners,)),
            dma((8,)), dma((8,)),
            dma((8,)), dma((8,)),
            dma((owners,)), dma((owners,)),
            dma((owners,)), dma((owners,)),
        ],
        compiler_params=pltpu.CompilerParams(
            collective_id=0, has_side_effects=True, vmem_limit_bytes=63 * 2**20
        ),
    )(passage_states, query_emb, head_weight, head_bias, norm_gain, candidate_ids)
    return pl.pallas_call(
        finish,
        out_shape=(jax.ShapeDtypeStruct((queries,), F32), jax.ShapeDtypeStruct((queries, width), F32)),
        in_specs=[hbm, hbm],
        out_specs=(vmem, vmem),
        scratch_shapes=[pltpu.VMEM((queries, 128), F32), dma((2,))],
        compiler_params=pltpu.CompilerParams(vmem_limit_bytes=63 * 2**20),
    )(loss, grad)


def solution(mesh):
    split = P(("group", "shard", "mp"), None)
    in_specs = (split, split, P(), P(), P(), split)
    out_specs = (P(("group", "shard", "mp")), split)
    return jax.shard_map(local, mesh=mesh, in_specs=in_specs, out_specs=out_specs, check_vma=False)
```

```python
import functools
import math

import jax
import jax.numpy as jnp
from jax import lax
from jax.experimental import pallas as pl
from jax.experimental.pallas import tpu as pltpu
from jax.sharding import PartitionSpec as P

MESH = pl.DeviceIdType.MESH
NT = (((1,), (1,)), ((), ()))
LOW = -1e30
F32, BF16 = jnp.float32, jnp.bfloat16


def kernel(
    owners, rows, queries, cands,
    states_in, query_in, w_in, bias_in, gain_in, ids_in,
    loss_out, grad_out,
    states, query, w, bias, gain, raw_ids, query_half, ids,
    slab, qbuf, qmat, idbuf, cnt, score, both, part, parts, stat, stats,
    load_sems, us, ur, ns, nr, vs, vr, cs, cr, qs, qr, ds, dr, gs, gr, hs, hr, ts, tr, ps, pr,
):
    width = w.shape[0]
    half_width = width // 2
    half = rows // 1
    span = 4 * rows
    every = owners * queries
    two = 2 * queries
    scaling = 1.0 / math.sqrt(width)
    y, s, mp = lax.axis_index("group"), lax.axis_index("shard"), lax.axis_index("mp")
    x, z_hi = s // 4, lax.rem(s, 4)
    z = z_hi * 2 + mp // 2
    core, y_lo = lax.rem(mp, 2), lax.rem(y, 2)
    y_hi = y // 2
    me = x * 4 + y_hi
    lane = y_lo * 2 + core
    lane_across = lax.rem(lane + 2, 4)
    lane_twin = lane + 1 - 2 * core
    lane_twin_across = lax.rem(lane_twin + 2, 4)

    def at_z(level):
        return {"shard": x * 4 + level // 2, "mp": lax.rem(level, 2) * 2 + core}

    above, below = at_z(lax.rem(z + 1, 8)), at_z(lax.rem(z + 7, 8))
    across = {"group": y + 1 - 2 * y_lo}
    twin = {"mp": mp + 1 - 2 * core}

    def peer(p):
        return {"group": lax.rem(p, 4) * 2 + y_lo, "shard": p // 4 * 4 + z_hi}

    def beside(k):
        return x * 4 + lax.rem(y_hi + k, 4)

    def column_of(k):
        return lax.rem(x + k, 8)

    def other(k):
        return lax.rem(me + k, owners)

    loads = [
        pltpu.make_async_copy(src, dst, load_sems.at[i])
        for i, (src, dst) in enumerate(
            ((w_in, w), (states_in, states), (bias_in, bias), (gain_in, gain), (query_in, query), (ids_in, raw_ids))
        )
    ]
    for load in loads:
        load.start()

    barrier = pltpu.get_barrier_semaphore()

    def greet(device):
        pl.semaphore_signal(barrier, inc=1, device_id=device, device_id_type=MESH)

    greet(below)

    @pl.when(z < 7)
    def _():
        greet(above)

    greet(across)
    greet(twin)

    for k in range(1, 4):
        greet(peer(beside(k)))
    for k in range(1, 8):
        greet(peer(column_of(k) * 4 + y_hi))

    for load in loads:
        load.wait()
    hidden = jnp.dot(states[...], w[...], preferred_element_type=F32) + bias[...].reshape(1, width)
    centred = hidden - jnp.mean(hidden, axis=-1, keepdims=True)
    spread = jnp.mean(centred * centred, axis=-1, keepdims=True)
    normal = centred * lax.rsqrt(spread + 1e-05) * gain[...].reshape(1, width)
    slab[pl.ds(pl.multiple_of(z * span + lane * rows, rows), rows), :] = normal.astype(BF16)
    pl.semaphore_wait(barrier, 13 + (z > 0).astype(jnp.int32))

    def send(src, dst, send_sem, recv_sem, device):
        return pltpu.make_async_remote_copy(
            src_ref=src, dst_ref=dst, send_sem=send_sem, recv_sem=recv_sem, device_id=device, device_id_type=MESH,
        )

    def chunk(level, which, h):
        return slab.at[pl.ds(pl.multiple_of(level * span + which * rows + h * half, half), half), :]

    def up(level, h):
        c, sem = chunk(level, lane, h), level * 1 + h
        return send(c, c, us.at[sem], ur.at[sem], above)

    def down(level, h):
        c, sem = chunk(level, lane, h), level * 1 + h
        return send(c, c, ns.at[sem], nr.at[sem], below)

    def over(level, h, which):
        c, sem = chunk(level, which, h), level * 1 + h
        return send(c, c, vs.at[sem], vr.at[sem], across)

    def to_twin(level, h, which):
        c, sem = chunk(level, which, h), level * 2 + which // 2 * 1 + h
        return send(c, c, cs.at[sem], cr.at[sem], twin)

    def reach_up(level):
        return jnp.where(level >= 4, 3, 7 - level)

    def reach_down(level):
        return jnp.where(level >= 4, 4, level)

    for h in range(1):
        up(z, h).start()

        @pl.when(z > 0)
        def _(h=h):
            down(z, h).start()

    for h in range(1):
        over(z, h, lane).start()
        to_twin(z, h, lane).start()

    wide = query[...].astype(F32)
    query_half[...] = jnp.concatenate([wide[:, :half_width], wide[:, half_width:]], axis=0).astype(BF16)
    raw = raw_ids[...]
    line = lax.broadcasted_iota(jnp.int32, raw.shape, 0)
    column = lax.broadcasted_iota(jnp.int32, raw.shape, 1)
    ring_of = (raw >> 8) & 31
    y_of = raw >> 13
    z_of = (ring_of & 3) * 2 + ((raw >> 7) & 1)
    owner_of = (ring_of >> 2) * 4 + (y_of >> 1)
    key_of = (z_of * 2 + (y_of & 1)) * queries + line
    packed = jnp.where(column == 0, 2**20, 0) + owner_of * 2**14 + key_of * 2**7 + (raw & 127)
    ids[...] = jnp.full(ids.shape, 63 * 2**14, jnp.int32)
    ids[:, :cands] = packed

    def q_at(p):
        return pl.ds(pl.multiple_of(p * two, two), two)

    def d_at(p):
        return pl.ds(pl.multiple_of(p * 8, 8), 8)

    def q_copy(p, at):
        return send(query_half, qbuf.at[q_at(at), :], qs.at[p], qr.at[at], peer(p))

    def d_copy(p, at):
        return send(ids, idbuf.at[d_at(at), :], ds.at[p], dr.at[at], peer(p))

    def column_copies(column, target):
        q_four = qbuf.at[pl.ds(pl.multiple_of(column * 4 * two, 4 * two), 4 * two), :]
        d_four = idbuf.at[pl.ds(pl.multiple_of(column * 32, 32), 32), :]
        device = peer(target * 4 + y_hi)
        return (
            lambda: send(d_four, d_four, gs.at[target], gr.at[column], device),
            lambda: send(q_four, q_four, hs.at[target], hr.at[column], device),
        )

    def share():
        for k in (2, 1, 3):
            d_copy(beside(k), me).start()
            q_copy(beside(k), me).start()

    def share_column():
        for k in range(1, 4):
            p = beside(k)
            d_copy(p, p).wait_recv()
            q_copy(p, p).wait_recv()
        for which in (0, 1):
            for k in (4, 3, 5, 2, 6, 1, 7):
                column_copies(x, column_of(k))[which]().start()

    def await_columns():
        for k in range(1, 8):
            for copy in column_copies(column_of(k), column_of(k)):
                copy().wait_recv()

    qbuf[q_at(me), :] = query_half[...]
    idbuf[d_at(me), :] = ids[...]

    def multiplicity(j, carry):
        block = idbuf[d_at(j), :]
        sub = lax.broadcasted_iota(jnp.int32, (128, 128), 0)
        left_hot, right_hot = [], []
        for t in range(queries):
            row = block[t : t + 1, :]
            key = ((row & 0xFFFFF) >> 7) - me * 128
            value = jnp.where((row >> 20) > 0, 129.0, 1.0)
            left_hot.append(jnp.where(sub == key, value, 0.0).astype(BF16))
            right_hot.append(jnp.where(sub == (row & 127), 1.0, 0.0).astype(BF16))
        left_hot, right_hot = jnp.concatenate(left_hot, axis=1), jnp.concatenate(right_hot, axis=1)
        total = lax.dot_general(left_hot, right_hot, NT, preferred_element_type=F32)
        for hi in range(16):
            cnt[d_at(j), hi * 128 : hi * 128 + 128] = total[hi * 8 : hi * 8 + 8, :]
        return carry

    def rise(k, when):
        level = lax.rem(z - k + 16, 8)
        return when, level, k + 1 <= reach_up(level), up

    def fall(k):
        level = lax.rem(z + k, 8)
        return jnp.logical_and(z + k <= 7, k <= reach_down(level)), level, k + 1 <= reach_down(level), down

    ups = {k: rise(k, z >= k) for k in range(1, 8)}
    falls = {k: fall(k) for k in range(1, 5)}
    wraps = {k: rise(z + k, z + k <= 3) for k in range(1, 4)}
    arrivals = [
        ups[1], ups[2], falls[1], ups[3], falls[2], ups[4], falls[3],
        ups[5], ups[6], ups[7], wraps[1], wraps[2], falls[4], wraps[3],
    ]

    def arrive(event):
        when, level, goes_on, way = event

        @pl.when(when)
        def _():
            for h in range(1):
                way(level, h).wait_recv()

                @pl.when(goes_on)
                def _(h=h):
                    way(level, h).start()

                over(level, h, lane).start()
                to_twin(level, h, lane).start()

    def pass_on(level):
        for h in range(1):
            over(level, h, lane_across).wait_recv()
            to_twin(level, h, lane_across).start()

    def use(level):
        for which in (lane_twin, lane_twin_across):
            for h in range(1):
                to_twin(level, h, which).wait_recv()
        at = pl.ds(pl.multiple_of(level * span, span), span)
        score[:, at] = lax.dot_general(qmat[...], slab[at, :], NT, preferred_element_type=F32) * scaling

    def later(event, do):
        @pl.when(event[0])
        def _():
            do(event[1])

    arrive(arrivals[0])
    share()

    def count(step, steps):
        lax.fori_loop(step * owners // steps, (step + 1) * owners // steps, multiplicity, 0, unroll=4)

    def widen():
        halves = qbuf[...].astype(F32).reshape(owners, 2, queries, half_width)
        qmat[:, :half_width] = halves[:, 0].reshape(every, half_width).astype(BF16)
        qmat[:, half_width:] = halves[:, 1].reshape(every, half_width).astype(BF16)

    order = [(True, z)] + arrivals
    upper, met = z >= 4, 12
    lower = jnp.logical_not(upper)
    for i in range(2, len(order)):
        arrive(order[i])
        if i == 9:
            later((jnp.logical_and(upper, order[7][0]), order[7][1]), pass_on)
        else:
            later(order[i - 2], pass_on)
        if i == 3:
            share_column()
        if 7 <= i <= 10:

            @pl.when(upper)
            def _(i=i):
                if i == 7:
                    await_columns()
                count(i - 7, 4)
                if i == 10:
                    widen()

        if i == 9:

            @pl.when(lower)
            def _():
                await_columns()
                count(0, 2)

        if i == met:
            later((jnp.logical_and(lower, order[7][0]), order[7][1]), pass_on)

            @pl.when(lower)
            def _():
                count(1, 2)
                widen()

            for event in order[: met - 3]:
                later(event, use)
        if i > met:
            later(order[i - 4], use)
    for event in order[-2:]:
        later(event, pass_on)
    for event in order[-4:]:
        later(event, use)

    batch = owners // 4
    per_batch = batch * queries // 16

    def softmax(i, carry):
        at = pl.ds(pl.multiple_of(i * 16, 16), 16)
        c = cnt[at, :]
        v = score[at, :]
        positive = c >= 128.0
        times = jnp.where(positive, c - 128.0, c)
        inside = jnp.where(times > 0.0, v, LOW)
        top = jnp.max(inside, axis=1, keepdims=True)
        e = times * jnp.exp(inside - top)
        total = jnp.sum(e, axis=1, keepdims=True)
        named = jnp.sum(jnp.where(positive, v, 0.0), axis=1, keepdims=True)
        put = pl.multiple_of(i // per_batch * 2 * batch * queries + lax.rem(i, per_batch) * 16, 16)
        both[pl.ds(put, 16), :] = e.astype(BF16)
        both[pl.ds(pl.multiple_of(put + batch * queries, 16), 16), :] = jnp.where(positive, 1.0, 0.0).astype(BF16)
        spot = lax.broadcasted_iota(jnp.int32, (16, 128), 1) - (lax.broadcasted_iota(jnp.int32, (16, 128), 0) & 7)
        tile = jnp.where(spot == 0, top, jnp.where(spot == 8, total, jnp.where(spot == 16, named, 0.0)))
        stat[pl.ds(i * 2, 2), :, :] = jnp.sum(tile.reshape(2, 8, 128), axis=1, keepdims=True)
        return carry

    lax.fori_loop(0, every // 16, softmax, 0, unroll=4)

    def t_copy(p, at):
        return send(stat.at[p], stats.at[at], ts.at[p], tr.at[at], peer(p))

    def tell(k, carry):
        t_copy(other(k), me).start()
        return carry

    stats[pl.ds(me, 1), :, :] = stat[pl.ds(me, 1), :, :]

    def p_at(p):
        return pl.ds(pl.multiple_of(p * 2 * two, 2 * two), 2 * two)

    def p_copy(p, frm, at):
        return send(part.at[p_at(frm), :], parts.at[p_at(at), :], ps.at[p], pr.at[at], peer(p))

    def partials(i, carry):
        b = lax.rem(x // 2 + jnp.where(i == 0, 2, jnp.where(i == 1, 1, jnp.where(i == 2, 3, 0))), 4)
        take = pl.ds(pl.multiple_of(b * 2 * batch * queries, 2 * batch * queries), 2 * batch * queries)
        sums = jnp.dot(both[take, :], slab[...], preferred_element_type=F32)
        pieces = [
            sums[i * batch * queries : (i + 1) * batch * queries, j * half_width : (j + 1) * half_width].reshape(
                batch, queries, half_width
            )
            for i in (0, 1)
            for j in (0, 1)
        ]
        put = pl.ds(pl.multiple_of(b * batch * 2 * two, batch * 2 * two), batch * 2 * two)
        part[put, :] = jnp.concatenate(pieces, axis=1).reshape(batch * 2 * two, half_width).astype(BF16)

        def give(pairs):
            def one(k, inner):
                for pair in pairs:
                    p = lax.rem(x // 2 + pair, 4) * batch + lax.rem(k, 2) * 4 + lax.rem(y_hi + 2 + 3 * (k // 2), 4)

                    @pl.when(p != me)
                    def _(p=p):
                        p_copy(p, p, me).start()

                return inner

            lax.fori_loop(0, batch, one, 0)

        @pl.when(i == 1)
        def _():
            lax.fori_loop(1, owners, tell, 0)

        for step, pairs in ((0, (2,)), (2, (1, 3)), (3, (0,))):

            @pl.when(i == step)
            def _(pairs=pairs):
                give(pairs)

        return carry

    lax.fori_loop(0, 4, partials, 0)
    parts[p_at(me), :] = part[p_at(me), :]

    def sent(k, carry):
        p = other(k)
        t_copy(p, me).wait_send()
        p_copy(p, p, me).wait_send()
        return carry

    lax.fori_loop(1, owners, sent, 0)

    for k in range(1, 4):
        d_copy(beside(k), me).wait_send()
        q_copy(beside(k), me).wait_send()
    for k in range(1, 8):
        for copy in column_copies(x, column_of(k)):
            copy().wait_send()

    def sent_rows(level, carry):
        risen, fallen = lax.rem(z - level + 8, 8), level - z

        @pl.when(risen + 1 <= reach_up(level))
        def _():
            for h in range(1):
                up(level, h).wait_send()

        @pl.when(jnp.logical_and(fallen >= 0, fallen + 1 <= reach_down(level)))
        def _():
            for h in range(1):
                down(level, h).wait_send()

        for h in range(1):
            over(level, h, lane).wait_send()
            to_twin(level, h, lane).wait_send()
            to_twin(level, h, lane_across).wait_send()
        return carry

    lax.fori_loop(0, 8, sent_rows, 0)

    def told(k, carry):
        t_copy(other(k), other(k)).wait_recv()
        return carry

    lax.fori_loop(1, owners, told, 0)
    told_all = stats[...].reshape(owners, 128)
    top = jnp.max(told_all, axis=0, keepdims=True)
    fade = jnp.exp(jnp.minimum(told_all - top, 0.0))
    total = jnp.sum(pltpu.roll(told_all, 120, 1) * fade, axis=0, keepdims=True)
    named = jnp.sum(pltpu.roll(told_all, 112, 1), axis=0, keepdims=True)
    own_spot = lax.broadcasted_iota(jnp.int32, (1, queries, 128), 2) == lax.broadcasted_iota(
        jnp.int32, (1, queries, 128), 1
    )

    def upright(flat):
        return jnp.sum(jnp.where(own_spot, flat.reshape(-1, 1, 128), 0.0), axis=2, keepdims=True)

    factor = upright(fade / total)
    loss_out[...] = jnp.broadcast_to(top + jnp.log(total) - named, (queries, 128))

    def taken(k, carry):
        p = other(k)
        p_copy(p, p, p).wait_recv()
        return carry

    lax.fori_loop(1, owners, taken, 0)
    got = parts[...].astype(F32).reshape(owners, 4, queries, half_width)
    for i in (0, 1):
        mean_row = jnp.sum(got[:, i] * factor, axis=0)
        grad_out[:, i * half_width : (i + 1) * half_width] = (mean_row - jnp.sum(got[:, 2 + i], axis=0)) * scaling


def finish(loss_in, grad_in, loss_out, grad_out, loss, sems):
    copies = [
        pltpu.make_async_copy(loss_in, loss, sems.at[0]),
        pltpu.make_async_copy(grad_in, grad_out, sems.at[1]),
    ]
    for copy in copies:
        copy.start()
    for copy in copies:
        copy.wait()
    loss_out[...] = loss[0, : loss_out.shape[0]]


def local(passage_states, query_emb, head_weight, head_bias, norm_gain, candidate_ids):
    owners = lax.axis_size("shard")
    rows, width = passage_states.shape
    queries, cands = candidate_ids.shape
    slab_rows = 8 * 4 * rows
    every = owners * queries
    dma = pltpu.SemaphoreType.DMA
    vmem = pl.BlockSpec(memory_space=pltpu.VMEM)
    hbm = pl.BlockSpec(memory_space=pltpu.HBM)
    loss, grad = pl.pallas_call(
        functools.partial(kernel, owners, rows, queries, cands),
        out_shape=(jax.ShapeDtypeStruct((queries, 128), F32), jax.ShapeDtypeStruct((queries, width), F32)),
        in_specs=[hbm] * 6,
        out_specs=(vmem, vmem),
        scratch_shapes=[
            pltpu.VMEM((rows, width), BF16),
            pltpu.VMEM((queries, width), BF16),
            pltpu.VMEM((width, width), BF16),
            pltpu.VMEM((width,), F32),
            pltpu.VMEM((width,), F32),
            pltpu.VMEM((queries, cands), jnp.int32),
            pltpu.VMEM((2 * queries, width // 2), BF16),
            pltpu.VMEM((8, 128), jnp.int32),
            pltpu.VMEM((slab_rows, width), BF16),
            pltpu.VMEM((2 * every, width // 2), BF16),
            pltpu.VMEM((every, width), BF16),
            pltpu.VMEM((owners * 8, 128), jnp.int32),
            pltpu.VMEM((every, slab_rows), F32),
            pltpu.VMEM((every, slab_rows), F32),
            pltpu.VMEM((2 * every, slab_rows), BF16),
            pltpu.VMEM((4 * every, width // 2), BF16),
            pltpu.VMEM((4 * every, width // 2), BF16),
            pltpu.VMEM((owners, 1, 128), F32),
            pltpu.VMEM((owners, 1, 128), F32),
            dma((6,)),
            dma((8,)), dma((8,)),
            dma((8,)), dma((8,)),
            dma((8,)), dma((8,)),
            dma((16,)), dma((16,)),
            dma((owners,)), dma((owners,)),
            dma((owners,)), dma((owners,)),
            dma((8,)), dma((8,)),
            dma((8,)), dma((8,)),
            dma((owners,)), dma((owners,)),
            dma((owners,)), dma((owners,)),
        ],
        compiler_params=pltpu.CompilerParams(
            collective_id=0, has_side_effects=True, vmem_limit_bytes=63 * 2**20
        ),
    )(passage_states, query_emb, head_weight, head_bias, norm_gain, candidate_ids)
    return pl.pallas_call(
        finish,
        out_shape=(jax.ShapeDtypeStruct((queries,), F32), jax.ShapeDtypeStruct((queries, width), F32)),
        in_specs=[hbm, hbm],
        out_specs=(vmem, vmem),
        scratch_shapes=[pltpu.VMEM((queries, 128), F32), dma((2,))],
        compiler_params=pltpu.CompilerParams(vmem_limit_bytes=63 * 2**20),
    )(loss, grad)


def solution(mesh):
    split = P(("group", "shard", "mp"), None)
    in_specs = (split, split, P(), P(), P(), split)
    out_specs = (P(("group", "shard", "mp")), split)
    return jax.shard_map(local, mesh=mesh, in_specs=in_specs, out_specs=out_specs, check_vma=False)
```

```python
import functools
import math

import jax
import jax.numpy as jnp
from jax import lax
from jax.experimental import pallas as pl
from jax.experimental.pallas import tpu as pltpu
from jax.sharding import PartitionSpec as P

MESH = pl.DeviceIdType.MESH
NT = (((1,), (1,)), ((), ()))
LOW = -1e30
F32, BF16 = jnp.float32, jnp.bfloat16


def kernel(
    owners, rows, queries, cands,
    states_in, query_in, w_in, bias_in, gain_in, ids_in,
    loss_out, grad_out,
    states, query, w, bias, gain, raw_ids, query_half, ids,
    slab, qbuf, qmat, idbuf, cnt, score, both, part, parts, stat, stats,
    load_sems, us, ur, ns, nr, vs, vr, cs, cr, qs, qr, ds, dr, gs, gr, hs, hr, ts, tr, ps, pr,
):
    width = w.shape[0]
    half_width = width // 2
    half = rows // 1
    span = 4 * rows
    every = owners * queries
    two = 2 * queries
    scaling = 1.0 / math.sqrt(width)
    y, s, mp = lax.axis_index("group"), lax.axis_index("shard"), lax.axis_index("mp")
    x, z_hi = s // 4, lax.rem(s, 4)
    z = z_hi * 2 + mp // 2
    core, y_lo = lax.rem(mp, 2), lax.rem(y, 2)
    y_hi = y // 2
    me = x * 4 + y_hi
    lane = y_lo * 2 + core
    lane_across = lax.rem(lane + 2, 4)
    lane_twin = lane + 1 - 2 * core
    lane_twin_across = lax.rem(lane_twin + 2, 4)

    def at_z(level):
        return {"shard": x * 4 + level // 2, "mp": lax.rem(level, 2) * 2 + core}

    above, below = at_z(lax.rem(z + 1, 8)), at_z(lax.rem(z + 7, 8))
    across = {"group": y + 1 - 2 * y_lo}
    twin = {"mp": mp + 1 - 2 * core}

    def peer(p):
        return {"group": lax.rem(p, 4) * 2 + y_lo, "shard": p // 4 * 4 + z_hi}

    def beside(k):
        return x * 4 + lax.rem(y_hi + k, 4)

    def column_of(k):
        return lax.rem(x + k, 8)

    def other(k):
        return lax.rem(me + k, owners)

    loads = [
        pltpu.make_async_copy(src, dst, load_sems.at[i])
        for i, (src, dst) in enumerate(
            ((w_in, w), (states_in, states), (bias_in, bias), (gain_in, gain), (query_in, query), (ids_in, raw_ids))
        )
    ]
    for load in loads:
        load.start()

    barrier = pltpu.get_barrier_semaphore()

    def greet(device):
        pl.semaphore_signal(barrier, inc=1, device_id=device, device_id_type=MESH)

    greet(below)

    @pl.when(z < 7)
    def _():
        greet(above)

    greet(across)
    greet(twin)

    for k in range(1, 4):
        greet(peer(beside(k)))
    for k in range(1, 8):
        greet(peer(column_of(k) * 4 + y_hi))

    for load in loads:
        load.wait()
    hidden = jnp.dot(states[...], w[...], preferred_element_type=F32) + bias[...].reshape(1, width)
    centred = hidden - jnp.mean(hidden, axis=-1, keepdims=True)
    spread = jnp.mean(centred * centred, axis=-1, keepdims=True)
    normal = centred * lax.rsqrt(spread + 1e-05) * gain[...].reshape(1, width)
    slab[pl.ds(pl.multiple_of(z * span + lane * rows, rows), rows), :] = normal.astype(BF16)
    pl.semaphore_wait(barrier, 13 + (z > 0).astype(jnp.int32))

    def send(src, dst, send_sem, recv_sem, device):
        return pltpu.make_async_remote_copy(
            src_ref=src, dst_ref=dst, send_sem=send_sem, recv_sem=recv_sem, device_id=device, device_id_type=MESH,
        )

    def chunk(level, which, h):
        return slab.at[pl.ds(pl.multiple_of(level * span + which * rows + h * half, half), half), :]

    def up(level, h):
        c, sem = chunk(level, lane, h), level * 1 + h
        return send(c, c, us.at[sem], ur.at[sem], above)

    def down(level, h):
        c, sem = chunk(level, lane, h), level * 1 + h
        return send(c, c, ns.at[sem], nr.at[sem], below)

    def over(level, h, which):
        c, sem = chunk(level, which, h), level * 1 + h
        return send(c, c, vs.at[sem], vr.at[sem], across)

    def to_twin(level, h, which):
        c, sem = chunk(level, which, h), level * 2 + which // 2 * 1 + h
        return send(c, c, cs.at[sem], cr.at[sem], twin)

    def reach_up(level):
        return jnp.where(level >= 4, 3, 7 - level)

    def reach_down(level):
        return jnp.where(level >= 4, 4, level)

    for h in range(1):
        up(z, h).start()

        @pl.when(z > 0)
        def _(h=h):
            down(z, h).start()

    for h in range(1):
        over(z, h, lane).start()
        to_twin(z, h, lane).start()

    wide = query[...].astype(F32)
    query_half[...] = jnp.concatenate([wide[:, :half_width], wide[:, half_width:]], axis=0).astype(BF16)
    raw = raw_ids[...]
    line = lax.broadcasted_iota(jnp.int32, raw.shape, 0)
    column = lax.broadcasted_iota(jnp.int32, raw.shape, 1)
    ring_of = (raw >> 8) & 31
    y_of = raw >> 13
    z_of = (ring_of & 3) * 2 + ((raw >> 7) & 1)
    owner_of = (ring_of >> 2) * 4 + (y_of >> 1)
    key_of = (z_of * 2 + (y_of & 1)) * queries + line
    packed = jnp.where(column == 0, 2**20, 0) + owner_of * 2**14 + key_of * 2**7 + (raw & 127)
    ids[...] = jnp.full(ids.shape, 63 * 2**14, jnp.int32)
    ids[:, :cands] = packed

    def q_at(p):
        return pl.ds(pl.multiple_of(p * two, two), two)

    def d_at(p):
        return pl.ds(pl.multiple_of(p * 8, 8), 8)

    def q_copy(p, at):
        return send(query_half, qbuf.at[q_at(at), :], qs.at[p], qr.at[at], peer(p))

    def d_copy(p, at):
        return send(ids, idbuf.at[d_at(at), :], ds.at[p], dr.at[at], peer(p))

    def column_copies(column, target):
        q_four = qbuf.at[pl.ds(pl.multiple_of(column * 4 * two, 4 * two), 4 * two), :]
        d_four = idbuf.at[pl.ds(pl.multiple_of(column * 32, 32), 32), :]
        device = peer(target * 4 + y_hi)
        return (
            lambda: send(d_four, d_four, gs.at[target], gr.at[column], device),
            lambda: send(q_four, q_four, hs.at[target], hr.at[column], device),
        )

    def share():
        for k in (2, 1, 3):
            d_copy(beside(k), me).start()
            q_copy(beside(k), me).start()

    def share_column():
        for k in range(1, 4):
            p = beside(k)
            d_copy(p, p).wait_recv()
            q_copy(p, p).wait_recv()
        for which in (0, 1):
            for k in (4, 3, 5, 2, 6, 1, 7):
                column_copies(x, column_of(k))[which]().start()

    def await_columns():
        for k in range(1, 8):
            for copy in column_copies(column_of(k), column_of(k)):
                copy().wait_recv()

    qbuf[q_at(me), :] = query_half[...]
    idbuf[d_at(me), :] = ids[...]

    def multiplicity(j, carry):
        block = idbuf[d_at(j), :]
        sub = lax.broadcasted_iota(jnp.int32, (128, 128), 0)
        left_hot, right_hot = [], []
        for t in range(queries):
            row = block[t : t + 1, :]
            key = ((row & 0xFFFFF) >> 7) - me * 128
            value = jnp.where((row >> 20) > 0, 129.0, 1.0)
            left_hot.append(jnp.where(sub == key, value, 0.0).astype(BF16))
            right_hot.append(jnp.where(sub == (row & 127), 1.0, 0.0).astype(BF16))
        left_hot, right_hot = jnp.concatenate(left_hot, axis=1), jnp.concatenate(right_hot, axis=1)
        total = lax.dot_general(left_hot, right_hot, NT, preferred_element_type=F32)
        for hi in range(16):
            cnt[d_at(j), hi * 128 : hi * 128 + 128] = total[hi * 8 : hi * 8 + 8, :]
        return carry

    def rise(k, when):
        level = lax.rem(z - k + 16, 8)
        return when, level, k + 1 <= reach_up(level), up

    def fall(k):
        level = lax.rem(z + k, 8)
        return jnp.logical_and(z + k <= 7, k <= reach_down(level)), level, k + 1 <= reach_down(level), down

    ups = {k: rise(k, z >= k) for k in range(1, 8)}
    falls = {k: fall(k) for k in range(1, 5)}
    wraps = {k: rise(z + k, z + k <= 3) for k in range(1, 4)}
    arrivals = [
        ups[1], ups[2], falls[1], ups[3], falls[2], ups[4], falls[3],
        ups[5], ups[6], ups[7], wraps[1], wraps[2], falls[4], wraps[3],
    ]

    def arrive(event):
        when, level, goes_on, way = event

        @pl.when(when)
        def _():
            for h in range(1):
                way(level, h).wait_recv()

                @pl.when(goes_on)
                def _(h=h):
                    way(level, h).start()

                over(level, h, lane).start()
                to_twin(level, h, lane).start()

    def pass_on(level):
        for h in range(1):
            over(level, h, lane_across).wait_recv()
            to_twin(level, h, lane_across).start()

    def use(level):
        for which in (lane_twin, lane_twin_across):
            for h in range(1):
                to_twin(level, h, which).wait_recv()
        at = pl.ds(pl.multiple_of(level * span, span), span)
        score[:, at] = lax.dot_general(qmat[...], slab[at, :], NT, preferred_element_type=F32) * scaling

    def later(event, do):
        @pl.when(event[0])
        def _():
            do(event[1])

    arrive(arrivals[0])
    share()

    def count(step, steps):
        lax.fori_loop(step * owners // steps, (step + 1) * owners // steps, multiplicity, 0, unroll=4)

    def widen():
        halves = qbuf[...].astype(F32).reshape(owners, 2, queries, half_width)
        qmat[:, :half_width] = halves[:, 0].reshape(every, half_width).astype(BF16)
        qmat[:, half_width:] = halves[:, 1].reshape(every, half_width).astype(BF16)

    order = [(True, z)] + arrivals
    upper, met = z >= 4, 12
    lower = jnp.logical_not(upper)
    for i in range(2, len(order)):
        arrive(order[i])
        if i == 9:
            later((jnp.logical_and(upper, order[7][0]), order[7][1]), pass_on)
        else:
            later(order[i - 2], pass_on)
        if i == 3:
            share_column()
        if 7 <= i <= 10:

            @pl.when(upper)
            def _(i=i):
                if i == 7:
                    await_columns()
                count(i - 7, 4)
                if i == 10:
                    widen()

        if i == 9:

            @pl.when(lower)
            def _():
                await_columns()
                count(0, 2)

        if i == met:
            later((jnp.logical_and(lower, order[7][0]), order[7][1]), pass_on)

            @pl.when(lower)
            def _():
                count(1, 2)
                widen()

            for event in order[: met - 3]:
                later(event, use)
        if i > met:
            later(order[i - 4], use)
    for event in order[-2:]:
        later(event, pass_on)
    for event in order[-4:]:
        later(event, use)

    batch = owners // 4
    per_batch = batch * queries // 16

    def softmax(i, carry):
        at = pl.ds(pl.multiple_of(i * 16, 16), 16)
        c = cnt[at, :]
        v = score[at, :]
        positive = c >= 128.0
        times = jnp.where(positive, c - 128.0, c)
        inside = jnp.where(times > 0.0, v, LOW)
        top = jnp.max(inside, axis=1, keepdims=True)
        e = times * jnp.exp(inside - top)
        total = jnp.sum(e, axis=1, keepdims=True)
        named = jnp.sum(jnp.where(positive, v, 0.0), axis=1, keepdims=True)
        put = pl.multiple_of(i // per_batch * 2 * batch * queries + lax.rem(i, per_batch) * 16, 16)
        both[pl.ds(put, 16), :] = e.astype(BF16)
        both[pl.ds(pl.multiple_of(put + batch * queries, 16), 16), :] = jnp.where(positive, 1.0, 0.0).astype(BF16)
        spot = lax.broadcasted_iota(jnp.int32, (16, 128), 1) - (lax.broadcasted_iota(jnp.int32, (16, 128), 0) & 7)
        tile = jnp.where(spot == 0, top, jnp.where(spot == 8, total, jnp.where(spot == 16, named, 0.0)))
        stat[pl.ds(i * 2, 2), :, :] = jnp.sum(tile.reshape(2, 8, 128), axis=1, keepdims=True)
        return carry


    def t_copy(p, at):
        return send(stat.at[p], stats.at[at], ts.at[p], tr.at[at], peer(p))

    def p_at(p):
        return pl.ds(pl.multiple_of(p * 2 * two, 2 * two), 2 * two)

    def p_copy(p, frm, at):
        return send(part.at[p_at(frm), :], parts.at[p_at(at), :], ps.at[p], pr.at[at], peer(p))

    def partials(i, carry):
        b = lax.rem(x // 2 + jnp.where(i == 0, 2, jnp.where(i == 1, 1, jnp.where(i == 2, 3, 0))), 4)
        lax.fori_loop(0, per_batch, lambda t, c: softmax(b * per_batch + t, c), 0, unroll=4)
        take = pl.ds(pl.multiple_of(b * 2 * batch * queries, 2 * batch * queries), 2 * batch * queries)
        sums = jnp.dot(both[take, :], slab[...], preferred_element_type=F32)
        pieces = [
            sums[i * batch * queries : (i + 1) * batch * queries, j * half_width : (j + 1) * half_width].reshape(
                batch, queries, half_width
            )
            for i in (0, 1)
            for j in (0, 1)
        ]
        put = pl.ds(pl.multiple_of(b * batch * 2 * two, batch * 2 * two), batch * 2 * two)
        part[put, :] = jnp.concatenate(pieces, axis=1).reshape(batch * 2 * two, half_width).astype(BF16)

        def give(pairs):
            def one(k, inner):
                for pair in pairs:
                    p = lax.rem(x // 2 + pair, 4) * batch + lax.rem(k, 2) * 4 + lax.rem(y_hi + 2 + 3 * (k // 2), 4)

                    @pl.when(p != me)
                    def _(p=p):
                        p_copy(p, p, me).start()
                        t_copy(p, me).start()

                return inner

            lax.fori_loop(0, batch, one, 0)

        for step, pairs in ((0, (2,)), (2, (1, 3)), (3, (0,))):

            @pl.when(i == step)
            def _(pairs=pairs):
                give(pairs)

        return carry

    lax.fori_loop(0, 4, partials, 0)
    parts[p_at(me), :] = part[p_at(me), :]
    stats[pl.ds(me, 1), :, :] = stat[pl.ds(me, 1), :, :]

    def sent(k, carry):
        p = other(k)
        t_copy(p, me).wait_send()
        p_copy(p, p, me).wait_send()
        return carry

    lax.fori_loop(1, owners, sent, 0)

    for k in range(1, 4):
        d_copy(beside(k), me).wait_send()
        q_copy(beside(k), me).wait_send()
    for k in range(1, 8):
        for copy in column_copies(x, column_of(k)):
            copy().wait_send()

    def sent_rows(level, carry):
        risen, fallen = lax.rem(z - level + 8, 8), level - z

        @pl.when(risen + 1 <= reach_up(level))
        def _():
            for h in range(1):
                up(level, h).wait_send()

        @pl.when(jnp.logical_and(fallen >= 0, fallen + 1 <= reach_down(level)))
        def _():
            for h in range(1):
                down(level, h).wait_send()

        for h in range(1):
            over(level, h, lane).wait_send()
            to_twin(level, h, lane).wait_send()
            to_twin(level, h, lane_across).wait_send()
        return carry

    lax.fori_loop(0, 8, sent_rows, 0)

    def told(k, carry):
        t_copy(other(k), other(k)).wait_recv()
        return carry

    lax.fori_loop(1, owners, told, 0)
    told_all = stats[...].reshape(owners, 128)
    top = jnp.max(told_all, axis=0, keepdims=True)
    fade = jnp.exp(jnp.minimum(told_all - top, 0.0))
    total = jnp.sum(pltpu.roll(told_all, 120, 1) * fade, axis=0, keepdims=True)
    named = jnp.sum(pltpu.roll(told_all, 112, 1), axis=0, keepdims=True)
    own_spot = lax.broadcasted_iota(jnp.int32, (1, queries, 128), 2) == lax.broadcasted_iota(
        jnp.int32, (1, queries, 128), 1
    )

    def upright(flat):
        return jnp.sum(jnp.where(own_spot, flat.reshape(-1, 1, 128), 0.0), axis=2, keepdims=True)

    factor = upright(fade / total)
    loss_out[...] = jnp.broadcast_to(top + jnp.log(total) - named, (queries, 128))

    def taken(k, carry):
        p = other(k)
        p_copy(p, p, p).wait_recv()
        return carry

    lax.fori_loop(1, owners, taken, 0)
    got = parts[...].astype(F32).reshape(owners, 4, queries, half_width)
    for i in (0, 1):
        mean_row = jnp.sum(got[:, i] * factor, axis=0)
        grad_out[:, i * half_width : (i + 1) * half_width] = (mean_row - jnp.sum(got[:, 2 + i], axis=0)) * scaling


def finish(loss_in, grad_in, loss_out, grad_out, loss, sems):
    copies = [
        pltpu.make_async_copy(loss_in, loss, sems.at[0]),
        pltpu.make_async_copy(grad_in, grad_out, sems.at[1]),
    ]
    for copy in copies:
        copy.start()
    for copy in copies:
        copy.wait()
    loss_out[...] = loss[0, : loss_out.shape[0]]


def local(passage_states, query_emb, head_weight, head_bias, norm_gain, candidate_ids):
    owners = lax.axis_size("shard")
    rows, width = passage_states.shape
    queries, cands = candidate_ids.shape
    slab_rows = 8 * 4 * rows
    every = owners * queries
    dma = pltpu.SemaphoreType.DMA
    vmem = pl.BlockSpec(memory_space=pltpu.VMEM)
    hbm = pl.BlockSpec(memory_space=pltpu.HBM)
    loss, grad = pl.pallas_call(
        functools.partial(kernel, owners, rows, queries, cands),
        out_shape=(jax.ShapeDtypeStruct((queries, 128), F32), jax.ShapeDtypeStruct((queries, width), F32)),
        in_specs=[hbm] * 6,
        out_specs=(vmem, vmem),
        scratch_shapes=[
            pltpu.VMEM((rows, width), BF16),
            pltpu.VMEM((queries, width), BF16),
            pltpu.VMEM((width, width), BF16),
            pltpu.VMEM((width,), F32),
            pltpu.VMEM((width,), F32),
            pltpu.VMEM((queries, cands), jnp.int32),
            pltpu.VMEM((2 * queries, width // 2), BF16),
            pltpu.VMEM((8, 128), jnp.int32),
            pltpu.VMEM((slab_rows, width), BF16),
            pltpu.VMEM((2 * every, width // 2), BF16),
            pltpu.VMEM((every, width), BF16),
            pltpu.VMEM((owners * 8, 128), jnp.int32),
            pltpu.VMEM((every, slab_rows), F32),
            pltpu.VMEM((every, slab_rows), F32),
            pltpu.VMEM((2 * every, slab_rows), BF16),
            pltpu.VMEM((4 * every, width // 2), BF16),
            pltpu.VMEM((4 * every, width // 2), BF16),
            pltpu.VMEM((owners, 1, 128), F32),
            pltpu.VMEM((owners, 1, 128), F32),
            dma((6,)),
            dma((8,)), dma((8,)),
            dma((8,)), dma((8,)),
            dma((8,)), dma((8,)),
            dma((16,)), dma((16,)),
            dma((owners,)), dma((owners,)),
            dma((owners,)), dma((owners,)),
            dma((8,)), dma((8,)),
            dma((8,)), dma((8,)),
            dma((owners,)), dma((owners,)),
            dma((owners,)), dma((owners,)),
        ],
        compiler_params=pltpu.CompilerParams(
            collective_id=0, has_side_effects=True, vmem_limit_bytes=63 * 2**20
        ),
    )(passage_states, query_emb, head_weight, head_bias, norm_gain, candidate_ids)
    return pl.pallas_call(
        finish,
        out_shape=(jax.ShapeDtypeStruct((queries,), F32), jax.ShapeDtypeStruct((queries, width), F32)),
        in_specs=[hbm, hbm],
        out_specs=(vmem, vmem),
        scratch_shapes=[pltpu.VMEM((queries, 128), F32), dma((2,))],
        compiler_params=pltpu.CompilerParams(vmem_limit_bytes=63 * 2**20),
    )(loss, grad)


def solution(mesh):
    split = P(("group", "shard", "mp"), None)
    in_specs = (split, split, P(), P(), P(), split)
    out_specs = (P(("group", "shard", "mp")), split)
    return jax.shard_map(local, mesh=mesh, in_specs=in_specs, out_specs=out_specs, check_vma=False)
```
